128 devices in a mesh: cone: 8 (over x_lo, y), con: 16 (over z, x_hi, core).
Axes of the slice: x: 4 (x_hi: 2, x_lo: 2; x = x_hi * 2 + x_lo), y: 4, z: 4, core: 2. Of those that a mesh axis runs over, the one named last changes fastest.
Arguments:
- vectors: bfloat16 [8, 16384, 1024], P('cone', 'con'), may hold values from -0.1875 to 0.1875
- primal: bfloat16 [8, 1024, 1024], P('cone'), may hold values from -8 to 8, as said below
- dual_inverse: bfloat16 [8, 1024, 1024], P('cone'), may hold values from -8 to 8, as said below
- touches: int32 [8, 16], P('cone'), may hold values from 0 to 1, as said below
Outputs:
- slab: float32 [4096, 16384], P('cone', 'con')
The draws below stay inside these ranges and needn't reach their ends.
Inputs may be any that keep to these rules, and one draw needn't show every extreme that they name: `primal`: symmetric and positive definite in every cone. `dual_inverse`: symmetric and positive definite in every cone. Every constraint block touches at least one cone.
All inputs are finite; a program needn't handle non-finite values.
Results may differ from the reference program's by a relative error of at most 0.00079.
Values may be sent and summed in bfloat16 or wider, within the bound.
A program may use at most 128 MiB of HBM per device.

```python
import jax
import jax.numpy as jnp
from jax import lax

NC = 1024
CON_DEV = 1024
PANEL = 512
COLUMNS = 16384
CONES = 8
BLOCKS = 16
N_CONE = 8
N_CON = 16


def definite_draw(key, salt_value):
    base_key = jax.random.fold_in(key, salt_value)
    first_key, second_key = jax.random.split(base_key)
    spread = jax.random.normal(first_key, (CONES, NC, NC), jnp.float32)
    diagonal = jax.random.uniform(second_key, (CONES, NC), jnp.float32, 0.5, 1.0)
    gram = jnp.einsum('cik,cjk->cij', spread, spread, precision=lax.Precision.HIGHEST) / NC
    gram = (gram + jnp.swapaxes(gram, 1, 2)) * 0.5
    identity = jnp.eye(NC, dtype=jnp.float32)[None]
    return (gram + diagonal[:, :, None] * identity).astype(jnp.bfloat16)


def draw_vectors(key, part):
    base_key = jax.random.fold_in(key, 53)
    noise_key, common_key = jax.random.split(base_key)
    unit = jnp.float32(NC) ** (-0.5)
    common = jax.random.normal(common_key, (CONES, 1, NC), jnp.float32) * unit
    noise = jax.random.normal(noise_key, (CONES, COLUMNS, NC), jnp.float32) * unit
    mixed = noise + 0.5 * common
    return jnp.clip(mixed, -6.0 * unit, 6.0 * unit).astype(jnp.bfloat16)


def draw_primal(key, part):
    return definite_draw(key, 11)


def draw_dual_inverse(key, part):
    return definite_draw(key, 23)


def draw_touches(key, part):
    base_key = jax.random.fold_in(key, 37)
    level_key, entry_key, home_key = jax.random.split(base_key, 3)
    levels = jax.random.randint(level_key, (CONES, 1), 0, 5)
    threshold = jnp.power(2, levels)
    entries = jax.random.randint(entry_key, (CONES, BLOCKS), 0, 16)
    homes = jax.random.randint(home_key, (1, BLOCKS), 0, CONES)
    cone_ids = jnp.arange(CONES, dtype=jnp.int32)[:, None]
    return ((entries < threshold) | (cone_ids == homes)).astype(jnp.int32)


def setup_inputs(seed: int = 0) -> dict:
    splits = jax.random.split(jax.random.key(seed), 5)
    vectors = draw_vectors(jax.random.fold_in(splits[4], 71), 0)
    primal = draw_primal(jax.random.fold_in(splits[4], 71), 0)
    dual_inverse = draw_dual_inverse(jax.random.fold_in(splits[4], 71), 0)
    touches = draw_touches(jax.random.fold_in(splits[4], 71), 0)
    return {"vectors": vectors, "primal": primal, "dual_inverse": dual_inverse, "touches": touches}


def row_constraints(row_dev):
    positions = jnp.arange(PANEL * N_CONE, dtype=jnp.int32)
    return (positions // row_dev * CON_DEV + positions % row_dev).astype(jnp.int32)

def reference(vectors, primal, dual_inverse, touches):
    row_dev = PANEL * N_CONE // N_CON
    columns_total = CON_DEV * N_CON
    column_ids = jnp.arange(columns_total, dtype=jnp.int32)
    column_block = column_ids // CON_DEV
    keep_flags = touches[:, column_block].astype(vectors.dtype)
    masked = vectors * keep_flags[:, :, None]
    chosen = row_constraints(row_dev)

    def one_cone(running, inputs):
        cone_vectors, primal_block, dual_block = inputs
        row_vectors = cone_vectors[chosen]
        row_primal = jnp.dot(row_vectors.astype(jnp.float32), primal_block.astype(jnp.float32), preferred_element_type=jnp.float32).astype(jnp.bfloat16)
        row_dual = jnp.dot(row_vectors.astype(jnp.float32), dual_block.astype(jnp.float32), preferred_element_type=jnp.float32).astype(jnp.bfloat16)
        gram_primal = jnp.dot(row_primal.astype(jnp.float32), cone_vectors.T.astype(jnp.float32), preferred_element_type=jnp.float32)
        gram_dual = jnp.dot(row_dual.astype(jnp.float32), cone_vectors.T.astype(jnp.float32), preferred_element_type=jnp.float32)
        return (running + gram_primal * gram_dual, None)
    schur_slab, _unused = lax.scan(one_cone, jnp.zeros((PANEL * N_CONE, columns_total), jnp.float32), (masked, primal, dual_inverse))
    panel_block = schur_slab[:PANEL]
    pivot_source = panel_block[:, chosen[:PANEL]]
    pivot_matrix = (pivot_source + pivot_source.T) * 0.5
    lower_factor = jnp.linalg.cholesky(pivot_matrix)
    factor_rows = jax.scipy.linalg.solve_triangular(lower_factor, panel_block, lower=True)
    row_factor = factor_rows[:, chosen]
    updated = schur_slab - jnp.einsum('kr,kc->rc', row_factor, factor_rows, precision=lax.Precision.HIGHEST)
    pivot_column = (column_block < N_CON // N_CONE) & (column_ids % CON_DEV < row_dev)
    remaining = jnp.where(pivot_column[None, :], 0.0, updated)
    return jnp.concatenate([factor_rows, remaining[PANEL:]], axis=0)
```

```python
import jax
import jax.numpy as jnp
from jax import lax
from jax.experimental import pallas as pl
from jax.experimental.pallas import tpu as pltpu
from jax.sharding import PartitionSpec as P

PANEL = 512
HI = lax.Precision.HIGHEST
NB = 128

def tdot(a, b, prec=HI):
    return lax.dot_general(a, b, (((0,), (0,)), ((), ())), precision=prec, preferred_element_type=jnp.float32)

def micro(R, c):
    d = {}
    for j in range(8):
        col = jnp.broadcast_to(R[:, c + j:c + j + 1], (8, 128))
        for i in range(j, 8):
            d[i, j] = jnp.broadcast_to(col[i:i + 1, :], (8, 128))
    rows = []
    for i in range(8):
        rows.append([jnp.broadcast_to(R[i:i + 1, h * 128:(h + 1) * 128], (8, 128)) for h in range(2)])
    for j in range(8):
        inv = lax.rsqrt(d[j, j])
        l = {}
        for i in range(j + 1, 8):
            l[i] = d[i, j] * inv
        rows[j] = [x * inv for x in rows[j]]
        for k in range(j + 1, 8):
            for i in range(k, 8):
                d[i, k] = d[i, k] - l[i] * l[k]
        for i in range(j + 1, 8):
            rows[i] = [x - l[i] * y for x, y in zip(rows[i], rows[j])]
    sub = lax.broadcasted_iota(jnp.int32, (8, 128), 0)
    outs = []
    for h in range(2):
        u = rows[0][h]
        for i in range(1, 8):
            u = jnp.where(sub == i, rows[i][h], u)
        outs.append(u)
    return jnp.concatenate(outs, axis=1)

def diag_factor(W):
    lane = lax.broadcasted_iota(jnp.int32, (8, 128), 1)
    for p in range(16):
        R = W[8 * p:8 * p + 8, :]
        U = micro(R, 8 * p)
        W[8 * p:8 * p + 8, :] = U
        lo = 8 * (p + 1)
        if p < 15:
            full = tdot(U[:, :128], U)
            W[lo:, :] = W[lo:, :] - full[lo:, :]

def kern(a_ref, s_ref, o_ref, X, W):
    n = s_ref.shape[1]
    X[:, :512] = (a_ref[...] + a_ref[...].T) * 0.5
    X[:, 512:] = s_ref[...]
    eye = (lax.broadcasted_iota(jnp.int32, (128, 128), 0) == lax.broadcasted_iota(jnp.int32, (128, 128), 1)).astype(jnp.float32)
    for k in range(4):
        W[:, :128] = X[k * 128:(k + 1) * 128, k * 128:(k + 1) * 128]
        W[:, 128:] = eye
        diag_factor(W)
        inv = W[:, 128:]
        lo = (k + 1) * 128
        X[k * 128:lo, lo:] = lax.dot_general(inv, X[k * 128:lo, lo:], (((1,), (0,)), ((), ())), precision=HI, preferred_element_type=jnp.float32)
        if k < 3:
            X[lo:, lo:] = X[lo:, lo:] - tdot(X[k * 128:lo, lo:512], X[k * 128:lo, lo:])
    o_ref[...] = X[:, 512:]

def run(a, s):
    n = s.shape[1]
    return pl.pallas_call(kern, out_shape=jax.ShapeDtypeStruct((512, n), jnp.float32),
        scratch_shapes=[pltpu.VMEM((512, 512 + n), jnp.float32), pltpu.VMEM((128, 256), jnp.float32)],
        compiler_params=pltpu.CompilerParams(vmem_limit_bytes=48 << 20))(a, s)


def broadcast(value, axis, source):
    kept = jnp.where(lax.axis_index(axis) == source, value, 0).astype(value.dtype)
    return lax.psum(kept, axis)


def shards(vectors, primal, dual_inverse, touches):
    con_count = lax.axis_size("con")
    cone_count = lax.axis_size("cone")
    con_place = lax.axis_index("con")
    cone_place = lax.axis_index("cone")
    per_block = vectors.shape[1]
    row_dev = PANEL * cone_count // con_count
    owners = con_count // cone_count
    touched = touches[0]
    own_flag = lax.dynamic_index_in_dim(touched, con_place, 0, keepdims=False)
    own_vectors = vectors[0] * own_flag.astype(jnp.bfloat16)
    primal_block = primal[0]
    dual_block = dual_inverse[0]
    leading = own_vectors[:row_dev]
    local_primal = jnp.dot(leading, primal_block, preferred_element_type=jnp.float32).astype(
        jnp.bfloat16
    )
    local_dual = jnp.dot(leading, dual_block, preferred_element_type=jnp.float32).astype(
        jnp.bfloat16
    )
    row_primal, row_dual = (
        lax.all_gather(local_primal, "con", axis=0, tiled=True),
        lax.all_gather(local_dual, "con", axis=0, tiled=True),
    )
    contract = (((1,), (1,)), ((), ()))
    gram_primal = lax.dot_general(
        row_primal, own_vectors, contract, preferred_element_type=jnp.float32
    )
    gram_dual = lax.dot_general(row_dual, own_vectors, contract, preferred_element_type=jnp.float32)
    schur_slab = lax.psum_scatter(gram_primal * gram_dual, "cone", scatter_dimension=0, tiled=True)
    panel_block = broadcast(schur_slab, "cone", 0)
    leading_columns = panel_block[:, :row_dev]
    gathered = lax.all_gather(leading_columns, "con", axis=1, tiled=True)
    pivot_source = gathered[:, :PANEL]
    block_source = lax.dynamic_slice_in_dim(gathered, cone_place * PANEL, PANEL, 1)
    combined = jnp.concatenate([panel_block, block_source], axis=1)
    solved = run(pivot_source, combined)
    factor_rows = solved[:, :per_block]
    row_factor = solved[:, per_block:]
    updated = schur_slab - jnp.einsum(
        "kr,kc->rc", row_factor, factor_rows, precision=lax.Precision.HIGHEST
    )
    local_columns = jnp.arange(per_block, dtype=jnp.int32)
    pivot_column = (con_place < owners) & (local_columns < row_dev)
    remaining = jnp.where(pivot_column[None, :], 0.0, updated)
    return jnp.where(cone_place == 0, factor_rows, remaining)


def solution(mesh):
    in_specs = (
        P("cone", "con", None),
        P("cone", None, None),
        P("cone", None, None),
        P("cone", None),
    )
    out_specs = P("cone", "con")
    return jax.shard_map(shards, mesh=mesh, in_specs=in_specs, out_specs=out_specs, check_vma=False)
```

```python
import jax
import jax.numpy as jnp
from jax import lax
from jax.experimental import pallas as pl
from jax.experimental.pallas import tpu as pltpu
from jax.sharding import PartitionSpec as P

PANEL = 512
LEAD = 256
HI = lax.Precision.HIGHEST
F32 = jnp.float32
BF16 = jnp.bfloat16
MESH = pl.DeviceIdType.MESH
STOPS = (3, 6, 9)


def tdot(a, b):
    return lax.dot_general(
        a, b, (((0,), (0,)), ((), ())), precision=HI, preferred_element_type=F32
    )


def hdot(a, b):
    return lax.dot_general(
        a, b, (((1,), (0,)), ((), ())), precision=HI, preferred_element_type=F32
    )


def micro(block, first):
    d = {}
    for j in range(8):
        column = jnp.broadcast_to(block[:, first + j : first + j + 1], (8, 128))
        for i in range(j, 8):
            d[i, j] = jnp.broadcast_to(column[i : i + 1, :], (8, 128))
    rows = [
        [jnp.broadcast_to(block[i : i + 1, h * 128 : (h + 1) * 128], (8, 128)) for h in range(2)]
        for i in range(8)
    ]
    for j in range(8):
        inverse = lax.rsqrt(d[j, j])
        low = {i: d[i, j] * inverse for i in range(j + 1, 8)}
        rows[j] = [x * inverse for x in rows[j]]
        for k in range(j + 1, 8):
            for i in range(k, 8):
                d[i, k] = d[i, k] - low[i] * low[k]
        for i in range(j + 1, 8):
            rows[i] = [x - low[i] * y for x, y in zip(rows[i], rows[j])]
    place = lax.broadcasted_iota(jnp.int32, (8, 128), 0)
    halves = []
    for h in range(2):
        upper = rows[0][h]
        for i in range(1, 8):
            upper = jnp.where(place == i, rows[i][h], upper)
        halves.append(upper)
    return jnp.concatenate(halves, axis=1)


def diagonal_factor(work):
    for p in range(16):
        upper = micro(work[8 * p : 8 * p + 8, :], 8 * p)
        work[8 * p : 8 * p + 8, :] = upper
        low = 8 * (p + 1)
        if p < 15:
            change = tdot(upper[:, :128], upper)
            work[low:, :] = work[low:, :] - change[low:, :]


def solve(X, work):
    square = (128, 128)
    eye = lax.broadcasted_iota(jnp.int32, square, 0) == lax.broadcasted_iota(jnp.int32, square, 1)

    @pl.loop(0, 4)
    def _(k):
        here = pl.ds(pl.multiple_of(k * 128, 128), 128)
        work[:, :128] = X[here, here]
        work[:, 128:] = eye.astype(F32)
        diagonal_factor(work)
        X[here, :] = hdot(work[:, 128:], X[here, :])

        @pl.loop(k + 1, 4)
        def _(r):
            there = pl.ds(pl.multiple_of(r * 128, 128), 128)
            X[there, :] = X[there, :] - tdot(X[here, there], X[here, :])


def encode(h, chunk):
    rows, columns = h.shape
    cut = h.reshape(rows // chunk, chunk, columns)
    peak = jnp.max(jnp.abs(cut), axis=1)
    inverse = jnp.where(peak > 1e-33, 32767.0 / jnp.maximum(peak, 1e-33), 0.0)
    coded = jnp.round(cut * inverse[:, None, :]).astype(jnp.int16)
    return coded.reshape(rows, columns), peak * (1.0 / 32767.0)


def decode(coded, scale, chunk):
    rows, columns = coded.shape
    cut = coded.astype(F32).reshape(rows // chunk, chunk, columns)
    return (cut * scale[:, None, :]).reshape(rows, columns)


def kernel(
    t_ref, v_hbm, p_hbm, d_hbm, out_ref,
    rows, V, Pm, Dm, rp, rd, sendq, recvq, ssc, rsc, acc, panel, psc, pqr, pscr, spread, X, work,
    load_sem, g_recv, g_x, g_z, g_s, pr_send, prs_send, pr_recv, prs_recv, ag_send, ag_recv,
    bq_send, bs_send, bq_recv, bs_recv, c_recv, c_x, c_z, c_s,
):
    c = lax.axis_index("cone")
    b = lax.axis_index("con")
    z = b // 4
    xh = (b // 2) % 2
    core = b % 2
    x_peer = b + 2 - 4 * xh
    sibling = b + 1 - 2 * core
    z_peers = [lax.rem(b + 4 * k, 16) for k in (1, 2, 3)]

    lead = pltpu.make_async_copy(
        v_hbm.at[0, pl.ds(0, LEAD), :], rows.at[pl.ds(LEAD * b, LEAD), :], load_sem.at[0]
    )
    loads = [
        pltpu.make_async_copy(h.at[0], m, load_sem.at[k + 1])
        for k, (h, m) in enumerate(((p_hbm, Pm), (d_hbm, Dm), (v_hbm, V)))
    ]
    lead.start()
    for load in loads:
        load.start()

    barrier = pltpu.get_barrier_semaphore()
    for peer in [x_peer, sibling] + z_peers:
        pl.semaphore_signal(barrier, inc=1, device_id={"con": peer}, device_id_type=MESH)
    for s in range(1, 8):
        pl.semaphore_signal(
            barrier, inc=1, device_id={"cone": lax.rem(c + s, 8)}, device_id_type=MESH
        )
    pl.semaphore_wait(barrier, 12)

    def block_copy(slot, sem, peer):
        ref = rows.at[pl.ds(pl.multiple_of(LEAD * slot, LEAD), LEAD), :]
        return pltpu.make_async_remote_copy(
            src_ref=ref, dst_ref=ref, send_sem=sem, recv_sem=g_recv.at[slot],
            device_id={"con": peer}, device_id_type=MESH,
        )

    def to_sibling(slot):
        return block_copy(slot, g_s.at[slot // 2], sibling)

    def to_z(slot, which):
        return [block_copy(slot, g_z.at[which, k], z_peers[k]) for k in range(3)]

    lead.wait()
    to_x = block_copy(b, g_x, x_peer)
    to_x.start()
    for copy in to_z(b, 0):
        copy.start()
    to_sibling(b).start()

    block_copy(x_peer, g_x, x_peer).wait_recv()
    for copy in to_z(x_peer, 1):
        copy.start()
    to_sibling(x_peer).start()

    def arrive(a):
        @pl.when(a // 2 != z)
        def _():
            slot = 2 * a + core
            block_copy(slot, g_x, x_peer).wait_recv()
            to_sibling(slot).start()

    def arrive_sibling(a):
        block_copy(2 * a + 1 - core, g_x, x_peer).wait_recv()

    own_flag = t_ref[0, b].astype(F32)

    def grams(a, sink):
        here = pl.ds(pl.multiple_of(a * PANEL, PANEL), PANEL)
        first = t_ref[0, 2 * a].astype(F32) * own_flag
        second = t_ref[0, 2 * a + 1].astype(F32) * own_flag
        place = lax.broadcasted_iota(jnp.int32, (PANEL, 256), 0)
        flags = jnp.where(place < LEAD, first, second)

        @pl.loop(0, 4)
        def _(n):
            cs = pl.ds(pl.multiple_of(n * 256, 256), 256)
            rp[:, cs] = jnp.dot(rows[here, :], Pm[:, cs], preferred_element_type=F32).astype(BF16)
            rd[:, cs] = jnp.dot(rows[here, :], Dm[:, cs], preferred_element_type=F32).astype(BF16)

        contract = (((1,), (1,)), ((), ()))

        @pl.loop(0, 4)
        def _(n):
            cs = pl.ds(pl.multiple_of(n * 256, 256), 256)
            gp = lax.dot_general(rp[...], V[cs, :], contract, preferred_element_type=F32)
            gd = lax.dot_general(rd[...], V[cs, :], contract, preferred_element_type=F32)
            sink(cs, gp * gd * flags)

    def panel_sink(cs, h):
        acc[:, cs] = h
        coded, scale = encode(h, 8)
        sendq[0, :, cs] = coded
        psc[:, cs] = scale

    def piece(i, size):
        return pl.ds(pl.multiple_of(i * size, size), size)

    def panel_copy(s, slot):
        peer = lax.rem(c + s, 8)
        return (
            pltpu.make_async_remote_copy(
                src_ref=sendq.at[0, piece(peer, 64), :], dst_ref=pqr.at[slot],
                send_sem=pr_send.at[s], recv_sem=pr_recv.at[slot],
                device_id={"cone": peer}, device_id_type=MESH,
            ),
            pltpu.make_async_remote_copy(
                src_ref=psc.at[piece(peer, 8), :], dst_ref=pscr.at[slot],
                send_sem=prs_send.at[s], recv_sem=prs_recv.at[slot],
                device_id={"cone": peer}, device_id_type=MESH,
            ),
        )

    def sum_copy(s, slot):
        ref = panel.at[piece(slot, 64), :]
        return pltpu.make_async_remote_copy(
            src_ref=ref, dst_ref=ref, send_sem=ag_send.at[s], recv_sem=ag_recv.at[slot],
            device_id={"cone": lax.rem(c + s, 8)}, device_id_type=MESH,
        )

    def bulk_copy(a, slot):
        return (
            pltpu.make_async_remote_copy(
                src_ref=sendq.at[a], dst_ref=recvq.at[slot],
                send_sem=bq_send.at[a], recv_sem=bq_recv.at[slot],
                device_id={"cone": a}, device_id_type=MESH,
            ),
            pltpu.make_async_remote_copy(
                src_ref=ssc.at[a], dst_ref=rsc.at[slot],
                send_sem=bs_send.at[a], recv_sem=bs_recv.at[slot],
                device_id={"cone": a}, device_id_type=MESH,
            ),
        )

    def bulk_step(t):
        a = lax.rem(c + t, 8)
        follow = lax.rem(c + t + 1, 8)

        @pl.when((t < 8) & (follow != 0))
        def _():
            arrive(follow)

        @pl.when(a != 0)
        def _():
            arrive_sibling(a)

            def sink(cs, h):
                @pl.when(a == c)
                def _():
                    acc[:, cs] = h

                @pl.when(a != c)
                def _():
                    coded, scale = encode(h, 32)
                    sendq[a, :, cs] = coded
                    ssc[a, :, cs] = scale

            grams(a, sink)

            @pl.when(a != c)
            def _():
                for copy in bulk_copy(a, c):
                    copy.start()

    def bulk(low, high):
        @pl.loop(low, high)
        def _(t):
            bulk_step(t)

    def spread_copy(kind, slot, sem, peer):
        ref = spread.at[kind, slot]
        return pltpu.make_async_remote_copy(
            src_ref=ref, dst_ref=ref, send_sem=sem, recv_sem=c_recv.at[kind, slot],
            device_id={"con": peer}, device_id_type=MESH,
        )

    homes = [(0, 0), (c // 2, lax.rem(c, 2))]

    def spread_on(kind):
        for k in range(3):
            spread_copy(kind, core, c_z.at[kind, k], z_peers[k]).start()
        spread_copy(kind, core, c_s.at[kind], sibling).start()

    def spread_start(kind):
        z0, x0 = homes[kind]

        @pl.when((z == z0) & (xh == x0))
        def _():
            spread[kind, core] = panel[:, :LEAD]
            spread_copy(kind, core, c_x.at[kind], x_peer).start()
            spread_on(kind)

    def spread_relay(kind):
        z0, x0 = homes[kind]

        @pl.when((z == z0) & (xh != x0))
        def _():
            spread_copy(kind, core, c_x.at[kind], x_peer).wait_recv()
            spread_on(kind)

        @pl.when(z != z0)
        def _():
            spread_copy(kind, core, c_x.at[kind], x_peer).wait_recv()
            spread_copy(kind, core, c_s.at[kind], sibling).start()

    def spread_end(kind):
        z0, x0 = homes[kind]
        spread_copy(kind, core, c_s.at[kind], sibling).wait_send()

        @pl.when(z == z0)
        def _():
            for k in range(3):
                spread_copy(kind, core, c_z.at[kind, k], z_peers[k]).wait_send()

        @pl.when((z == z0) & (xh == x0))
        def _():
            spread_copy(kind, core, c_x.at[kind], x_peer).wait_send()

    arrive(0)
    arrive_sibling(0)
    for load in loads:
        load.wait()
    grams(0, panel_sink)
    for s in range(1, 8):
        for copy in panel_copy(s, c):
            copy.start()

    first = lax.rem(c + 1, 8)

    @pl.when(first != 0)
    def _():
        arrive(first)

    bulk(1, STOPS[0])

    mine = piece(c, 64)
    panel[mine, :] = acc[mine, :]

    @pl.loop(1, 8)
    def _(s):
        source = lax.rem(c + s, 8)
        for copy in panel_copy(s, source):
            copy.wait_recv()
        panel[mine, :] = panel[mine, :] + decode(pqr[source], pscr[source], 8)

    for s in range(1, 8):
        sum_copy(s, c).start()

    bulk(STOPS[0], STOPS[1])

    for s in range(1, 8):
        sum_copy(s, lax.rem(c + s, 8)).wait_recv()
    for kind in range(2):
        spread_start(kind)

    bulk(STOPS[1], STOPS[2])

    for kind in range(2):
        spread_relay(kind)
    for kind in range(2):
        spread_copy(kind, 1 - core, c_s.at[kind], sibling).wait_recv()
    bulk(STOPS[2], 9)

    X[:, :LEAD] = spread[0, 0]
    X[:, LEAD:PANEL] = spread[0, 1]
    pivot = X[:, :PANEL]
    X[:, :PANEL] = (pivot + pivot.T) * 0.5
    X[:, PANEL : PANEL + 1024] = panel[...]
    X[:, PANEL + 1024 : PANEL + 1024 + LEAD] = spread[1, 0]
    X[:, PANEL + 1024 + LEAD :] = spread[1, 1]
    solve(X, work)

    @pl.when(c != 0)
    def _():
        @pl.loop(1, 8)
        def _(s):
            source = lax.rem(c + s, 8)
            for copy in bulk_copy(source, source):
                copy.wait_recv()
            for r in range(4):
                part = pl.ds(r * 128, 128)
                acc[part, :] = acc[part, :] + decode(
                    recvq[source, part, :], rsc[source, pl.ds(r * 4, 4), :], 32
                )

        @pl.loop(0, 4)
        def _(r):
            part = pl.ds(pl.multiple_of(r * 128, 128), 128)
            columns = pl.ds(pl.multiple_of(PANEL + 1024 + r * 128, 128), 128)
            change = tdot(X[:, columns], X[:, PANEL : PANEL + 1024])
            place = lax.broadcasted_iota(jnp.int32, (128, 1024), 1)
            gone = (place < LEAD) & (b < 2)
            out_ref[part, :] = jnp.where(gone, 0.0, acc[part, :] - change)

    @pl.when(c == 0)
    def _():
        out_ref[...] = X[:, PANEL : PANEL + 1024]

    to_x.wait_send()
    for copy in to_z(b, 0) + to_z(x_peer, 1):
        copy.wait_send()

    @pl.loop(0, 8)
    def _(a):
        to_sibling(2 * a + core).wait_send()

    for s in range(1, 8):
        for copy in panel_copy(s, c):
            copy.wait_send()
        sum_copy(s, c).wait_send()

        a = lax.rem(c + s, 8)

        @pl.when(a != 0)
        def _():
            for copy in bulk_copy(a, c):
                copy.wait_send()

    for kind in range(2):
        spread_end(kind)


def shards(vectors, primal, dual_inverse, touches):
    dma = pltpu.SemaphoreType.DMA
    vmem = pltpu.VMEM
    anywhere = pl.BlockSpec(memory_space=pl.ANY)
    return pl.pallas_call(
        kernel,
        out_shape=jax.ShapeDtypeStruct((PANEL, 1024), F32),
        in_specs=[pl.BlockSpec(memory_space=pltpu.SMEM), anywhere, anywhere, anywhere],
        out_specs=pl.BlockSpec(memory_space=pltpu.VMEM),
        scratch_shapes=[
            vmem((4096, 1024), BF16),
            vmem((1024, 1024), BF16),
            vmem((1024, 1024), BF16),
            vmem((1024, 1024), BF16),
            vmem((PANEL, 1024), BF16),
            vmem((PANEL, 1024), BF16),
            vmem((8, PANEL, 1024), jnp.int16),
            vmem((8, PANEL, 1024), jnp.int16),
            vmem((8, 16, 1024), F32),
            vmem((8, 16, 1024), F32),
            vmem((PANEL, 1024), F32),
            vmem((PANEL, 1024), F32),
            vmem((64, 1024), F32),
            vmem((8, 64, 1024), jnp.int16),
            vmem((8, 8, 1024), F32),
            vmem((2, 2, PANEL, LEAD), F32),
            vmem((PANEL, 2048), F32),
            vmem((128, 256), F32),
            dma((4,)), dma((16,)), dma, dma((2, 3)), dma((8,)),
            dma((8,)), dma((8,)), dma((8,)), dma((8,)), dma((8,)), dma((8,)),
            dma((8,)), dma((8,)), dma((8,)), dma((8,)),
            dma((2, 2)), dma((2,)), dma((2, 3)), dma((2,)),
        ],
        compiler_params=pltpu.CompilerParams(
            collective_id=0, has_side_effects=True, vmem_limit_bytes=60 << 20
        ),
    )(touches, vectors, primal, dual_inverse)


def solution(mesh):
    in_specs = (
        P("cone", "con", None),
        P("cone", None, None),
        P("cone", None, None),
        P("cone", None),
    )
    out_specs = P("cone", "con")
    return jax.shard_map(shards, mesh=mesh, in_specs=in_specs, out_specs=out_specs, check_vma=False)
```

```python
import jax
import jax.numpy as jnp
from jax import lax
from jax.experimental import pallas as pl
from jax.experimental.pallas import tpu as pltpu
from jax.sharding import PartitionSpec as P

PANEL = 512
LEAD = 256
HI = lax.Precision.HIGHEST
F32 = jnp.float32
BF16 = jnp.bfloat16
MESH = pl.DeviceIdType.MESH
OFFSETS = ((0, 1), (0, 3), (1, 0), (0, 2), (1, 1), (1, 3), (1, 2), (0, 0))
FIRST_STEPS = 4
STEPS_PER_BLOCK = 2


def tdot(a, b):
    return lax.dot_general(
        a, b, (((0,), (0,)), ((), ())), precision=HI, preferred_element_type=F32
    )


def hdot(a, b):
    return lax.dot_general(
        a, b, (((1,), (0,)), ((), ())), precision=HI, preferred_element_type=F32
    )


def micro(block, first):
    d = {}
    for j in range(8):
        column = jnp.broadcast_to(block[:, first + j : first + j + 1], (8, 128))
        for i in range(j, 8):
            d[i, j] = jnp.broadcast_to(column[i : i + 1, :], (8, 128))
    rows = [
        [jnp.broadcast_to(block[i : i + 1, h * 128 : (h + 1) * 128], (8, 128)) for h in range(2)]
        for i in range(8)
    ]
    for j in range(8):
        inverse = lax.rsqrt(d[j, j])
        low = {i: d[i, j] * inverse for i in range(j + 1, 8)}
        rows[j] = [x * inverse for x in rows[j]]
        for k in range(j + 1, 8):
            for i in range(k, 8):
                d[i, k] = d[i, k] - low[i] * low[k]
        for i in range(j + 1, 8):
            rows[i] = [x - low[i] * y for x, y in zip(rows[i], rows[j])]
    place = lax.broadcasted_iota(jnp.int32, (8, 128), 0)
    halves = []
    for h in range(2):
        upper = rows[0][h]
        for i in range(1, 8):
            upper = jnp.where(place == i, rows[i][h], upper)
        halves.append(upper)
    return jnp.concatenate(halves, axis=1)


def diagonal_factor(work):
    for p in range(16):
        upper = micro(work[8 * p : 8 * p + 8, :], 8 * p)
        work[8 * p : 8 * p + 8, :] = upper
        low = 8 * (p + 1)
        if p < 15:
            change = tdot(upper[:, :128], upper)
            work[low:, :] = work[low:, :] - change[low:, :]


def block(i):
    return pl.ds(pl.multiple_of(i * 128, 128), 128)


def factor_step(k, A, inverses, work):
    square = (128, 128)
    eye = lax.broadcasted_iota(jnp.int32, square, 0) == lax.broadcasted_iota(jnp.int32, square, 1)
    here = block(k)
    work[:, :128] = A[here, here]
    work[:, 128:] = eye.astype(F32)
    diagonal_factor(work)
    inverses[k] = work[:, 128:]
    A[here, :] = hdot(work[:, 128:], A[here, :])

    @pl.loop(k + 1, 4)
    def _(r):
        A[block(r), :] = A[block(r), :] - tdot(A[here, block(r)], A[here, :])


def substitute(A, inverses, X):
    @pl.loop(0, 4)
    def _(k):
        here = block(k)
        X[here, :] = hdot(inverses[k], X[here, :])

        @pl.loop(k + 1, 4)
        def _(r):
            X[block(r), :] = X[block(r), :] - tdot(A[here, block(r)], X[here, :])


def encode(h, chunk):
    rows, columns = h.shape
    cut = h.reshape(rows // chunk, chunk, columns)
    peak = jnp.max(jnp.abs(cut), axis=1)
    inverse = jnp.where(peak > 1e-33, 32767.0 / jnp.maximum(peak, 1e-33), 0.0)
    coded = jnp.round(cut * inverse[:, None, :]).astype(jnp.int16)
    return coded.reshape(rows, columns), peak * (1.0 / 32767.0)


def decode(coded, scale, chunk):
    rows, columns = coded.shape
    cut = coded.astype(F32).reshape(rows // chunk, chunk, columns)
    return (cut * scale[:, None, :]).reshape(rows, columns)


def kernel(
    t_ref, v_hbm, p_hbm, d_hbm, out_ref,
    rows, V, Pm, Dm, rp, rd, sendq, recvq, ssc, rsc, acc, psc, pqr, pscr,
    bpart, brecv, bfull, A, inverses, X, work,
    load_sem, g_recv, g_x, g_z, g_s, pr_send, prs_send, pr_recv, prs_recv, ag_send, ag_recv,
    bq_send, bs_send, bq_recv, bs_recv, c_recv, c_x, c_z, c_s,
    br_send, br_recv, ba_send, ba_recv, bx_send, bx_recv,
):
    c = lax.axis_index("cone")
    b = lax.axis_index("con")
    z = b // 4
    xh = (b // 2) % 2
    core = b % 2
    x_peer = b + 2 - 4 * xh
    sibling = b + 1 - 2 * core
    z_peers = [lax.rem(b + 4 * k, 16) for k in (1, 2, 3)]

    lead = pltpu.make_async_copy(
        v_hbm.at[0, pl.ds(0, LEAD), :], rows.at[pl.ds(LEAD * b, LEAD), :], load_sem.at[0]
    )
    loads = [
        pltpu.make_async_copy(h.at[0], m, load_sem.at[k + 1])
        for k, (h, m) in enumerate(((p_hbm, Pm), (d_hbm, Dm), (v_hbm, V)))
    ]
    lead.start()
    for load in loads:
        load.start()

    barrier = pltpu.get_barrier_semaphore()
    for peer in [x_peer, sibling] + z_peers:
        pl.semaphore_signal(barrier, inc=1, device_id={"con": peer}, device_id_type=MESH)
    for s in range(1, 8):
        pl.semaphore_signal(
            barrier, inc=1, device_id={"cone": lax.rem(c + s, 8)}, device_id_type=MESH
        )
    pl.semaphore_wait(barrier, 12)

    def block_copy(slot, sem, peer):
        ref = rows.at[pl.ds(pl.multiple_of(LEAD * slot, LEAD), LEAD), :]
        return pltpu.make_async_remote_copy(
            src_ref=ref, dst_ref=ref, send_sem=sem, recv_sem=g_recv.at[slot],
            device_id={"con": peer}, device_id_type=MESH,
        )

    def to_sibling(slot):
        return block_copy(slot, g_s.at[slot // 2], sibling)

    def to_z(slot, which):
        return [block_copy(slot, g_z.at[which, k], z_peers[k]) for k in range(3)]

    lead.wait()
    to_x = block_copy(b, g_x, x_peer)
    to_x.start()
    for copy in to_z(b, 0):
        copy.start()
    to_sibling(b).start()

    def arrive(a):
        @pl.when(a // 2 != z)
        def _():
            slot = 2 * a + core
            block_copy(slot, g_x, x_peer).wait_recv()
            to_sibling(slot).start()

    def arrive_sibling(a):
        block_copy(2 * a + 1 - core, g_x, x_peer).wait_recv()

    own_flag = t_ref[0, b].astype(F32)

    own_chip = b // 2
    contract = (((1,), (1,)), ((), ()))

    def products(a):
        here = pl.ds(pl.multiple_of(a * PANEL, PANEL), PANEL)

        @pl.loop(0, 4)
        def _(n):
            cs = pl.ds(pl.multiple_of(n * 256, 256), 256)
            rp[:, cs] = jnp.dot(rows[here, :], Pm[:, cs], preferred_element_type=F32).astype(BF16)
            rd[:, cs] = jnp.dot(rows[here, :], Dm[:, cs], preferred_element_type=F32).astype(BF16)

    def grams(a, sink):
        first = t_ref[0, 2 * a].astype(F32) * own_flag
        second = t_ref[0, 2 * a + 1].astype(F32) * own_flag
        place = lax.broadcasted_iota(jnp.int32, (PANEL, 256), 0)
        flags = jnp.where(place < LEAD, first, second)

        @pl.loop(0, 4)
        def _(n):
            cs = pl.ds(pl.multiple_of(n * 256, 256), 256)
            gp = lax.dot_general(rp[...], V[cs, :], contract, preferred_element_type=F32)
            gd = lax.dot_general(rd[...], V[cs, :], contract, preferred_element_type=F32)
            sink(cs, gp * gd * flags)

    def piece(i, size):
        return pl.ds(pl.multiple_of(i * size, size), size)

    def pivot_part():
        half = piece(core, LEAD)
        row_flag = t_ref[0, core].astype(F32)
        place = lax.broadcasted_iota(jnp.int32, (LEAD, PANEL), 1)
        flags = jnp.where(place < LEAD, t_ref[0, 0].astype(F32), t_ref[0, 1].astype(F32)) * row_flag
        lead_rows = rows[:PANEL, :]
        gp = lax.dot_general(rp[half, :], lead_rows, contract, preferred_element_type=F32)
        gd = lax.dot_general(rd[half, :], lead_rows, contract, preferred_element_type=F32)
        bpart[...] = gp * gd * flags

    def pivot_copy(s, slot):
        peer = lax.rem(c + s, 8)
        return pltpu.make_async_remote_copy(
            src_ref=bpart.at[piece(peer, 32), :], dst_ref=brecv.at[slot],
            send_sem=br_send.at[s], recv_sem=br_recv.at[slot],
            device_id={"cone": peer}, device_id_type=MESH,
        )

    def pivot_sum_copy(s, slot):
        ref = bfull.at[core, piece(slot, 32), :]
        return pltpu.make_async_remote_copy(
            src_ref=ref, dst_ref=ref, send_sem=ba_send.at[s], recv_sem=ba_recv.at[slot],
            device_id={"cone": lax.rem(c + s, 8)}, device_id_type=MESH,
        )

    def pivot_half_copy(half):
        ref = bfull.at[half]
        return pltpu.make_async_remote_copy(
            src_ref=ref, dst_ref=ref, send_sem=bx_send, recv_sem=bx_recv,
            device_id={"con": sibling}, device_id_type=MESH,
        )

    def panel_sink(cs, h):
        X[:, cs] = h
        coded, scale = encode(h, 8)
        sendq[0, :, cs] = coded
        psc[:, cs] = scale

    def panel_copy(s, slot):
        peer = lax.rem(c + s, 8)
        return (
            pltpu.make_async_remote_copy(
                src_ref=sendq.at[0, piece(peer, 64), :], dst_ref=pqr.at[slot],
                send_sem=pr_send.at[s], recv_sem=pr_recv.at[slot],
                device_id={"cone": peer}, device_id_type=MESH,
            ),
            pltpu.make_async_remote_copy(
                src_ref=psc.at[piece(peer, 8), :], dst_ref=pscr.at[slot],
                send_sem=prs_send.at[s], recv_sem=prs_recv.at[slot],
                device_id={"cone": peer}, device_id_type=MESH,
            ),
        )

    def sum_copy(s, slot):
        ref = X.at[piece(slot, 64), pl.ds(0, 1024)]
        return pltpu.make_async_remote_copy(
            src_ref=ref, dst_ref=ref, send_sem=ag_send.at[s], recv_sem=ag_recv.at[slot],
            device_id={"cone": lax.rem(c + s, 8)}, device_id_type=MESH,
        )

    def bulk_copy(a, slot):
        return (
            pltpu.make_async_remote_copy(
                src_ref=sendq.at[a], dst_ref=recvq.at[slot],
                send_sem=bq_send.at[a], recv_sem=bq_recv.at[slot],
                device_id={"cone": a}, device_id_type=MESH,
            ),
            pltpu.make_async_remote_copy(
                src_ref=ssc.at[a], dst_ref=rsc.at[slot],
                send_sem=bs_send.at[a], recv_sem=bs_recv.at[slot],
                device_id={"cone": a}, device_id_type=MESH,
            ),
        )

    def bulk_part(a, part):
        here = pl.ds(128 * part, 128)
        return pltpu.make_async_remote_copy(
            src_ref=sendq.at[a, here, :], dst_ref=recvq.at[c, here, :],
            send_sem=bq_send.at[a], recv_sem=bq_recv.at[c],
            device_id={"cone": a}, device_id_type=MESH,
        )

    def compute(a):
        def sink(cs, h):
            @pl.when(a == c)
            def _():
                acc[:, cs] = h

            @pl.when(a != c)
            def _():
                coded, scale = encode(h, 32)
                sendq[a, :, cs] = coded
                ssc[a, :, cs] = scale

        arrive_sibling(a)
        products(a)
        grams(a, sink)

    def target(t):
        dx = dy = 0
        for k, (x, y) in enumerate(OFFSETS):
            dx = jnp.where(t == k + 1, x, dx)
            dy = jnp.where(t == k + 1, y, dy)
        return lax.rem(c // 4 + dx, 2) * 4 + lax.rem(lax.rem(c, 4) + dy, 4)

    def issue(low, high):
        for part in range(4):
            for t in range(low, high):
                a = target(t)

                @pl.when(a != 0)
                def _():
                    if part == 0:
                        bulk_copy(a, c)[1].start()
                    bulk_part(a, part).start()

    def bulk_step(t):
        a = target(t)
        follow = target(t + 1)

        @pl.when((t < 8) & (follow != 0))
        def _():
            arrive(follow)

        @pl.when((a != 0) & (a != own_chip))
        def _():
            compute(a)

        @pl.when((t == 3))
        def _():
            issue(1, 4)

        @pl.when((t == 7))
        def _():
            issue(4, 8)

    def bulk(low, high):
        @pl.loop(low, high)
        def _(t):
            bulk_step(t)

    def spread_copy(slot, sem, peer):
        ref = X.at[:, pl.ds(pl.multiple_of(1024 + slot * LEAD, LEAD), LEAD)]
        return pltpu.make_async_remote_copy(
            src_ref=ref, dst_ref=ref, send_sem=sem, recv_sem=c_recv.at[slot],
            device_id={"con": peer}, device_id_type=MESH,
        )

    at_home_z = z == c // 2
    at_home_x = xh == lax.rem(c, 2)

    def spread_on():
        for k in range(3):
            spread_copy(core, c_z.at[k], z_peers[k]).start()
        spread_copy(core, c_s, sibling).start()

    def spread_start():
        @pl.when(at_home_z & at_home_x)
        def _():
            X[:, pl.ds(pl.multiple_of(1024 + core * LEAD, LEAD), LEAD)] = X[:, :LEAD]
            spread_copy(core, c_x, x_peer).start()
            spread_on()

    def spread_relay():
        @pl.when(at_home_z & (xh != lax.rem(c, 2)))
        def _():
            spread_copy(core, c_x, x_peer).wait_recv()
            spread_on()

    def spread_relay_far():
        @pl.when(z != c // 2)
        def _():
            spread_copy(core, c_x, x_peer).wait_recv()
            spread_copy(core, c_s, sibling).start()

    def spread_end():
        spread_copy(core, c_s, sibling).wait_send()

        @pl.when(at_home_z)
        def _():
            for k in range(3):
                spread_copy(core, c_z.at[k], z_peers[k]).wait_send()

        @pl.when(at_home_z & at_home_x)
        def _():
            spread_copy(core, c_x, x_peer).wait_send()

    for load in loads:
        load.wait()

    @pl.when(own_chip != 0)
    def _():
        compute(own_chip)

    block_copy(x_peer, g_x, x_peer).wait_recv()
    for copy in to_z(x_peer, 1):
        copy.start()
    to_sibling(x_peer).start()

    arrive(0)
    arrive_sibling(0)
    products(0)
    pivot_part()
    for s in range(1, 8):
        pivot_copy(s, c).start()

    grams(0, panel_sink)

    half_piece = piece(c, 32)
    bfull[core, half_piece, :] = bpart[half_piece, :]

    @pl.loop(1, 8)
    def _(s):
        source = lax.rem(c + s, 8)
        pivot_copy(s, source).wait_recv()
        bfull[core, half_piece, :] = bfull[core, half_piece, :] + brecv[source]

    for s in range(1, 8):
        pivot_sum_copy(s, c).start()
    for s in range(1, 8):
        for copy in panel_copy(s, c):
            copy.start()

    follow = target(1)

    @pl.when(follow != 0)
    def _():
        arrive(follow)

    bulk(1, FIRST_STEPS)

    for s in range(1, 8):
        pivot_sum_copy(s, lax.rem(c + s, 8)).wait_recv()
    pivot_half_copy(core).start()

    mine = piece(c, 64)

    @pl.loop(1, 8)
    def _(s):
        source = lax.rem(c + s, 8)
        for copy in panel_copy(s, source):
            copy.wait_recv()
        X[mine, :1024] = X[mine, :1024] + decode(pqr[source], pscr[source], 8)

    for s in range(1, 8):
        sum_copy(s, c).start()

    pivot_half_copy(1 - core).wait_recv()
    A[:LEAD, :] = bfull[0]
    A[LEAD:, :] = bfull[1]
    A[...] = (A[...] + A[...].T) * 0.5

    @pl.loop(0, 4)
    def _(k):
        factor_step(k, A, inverses, work)

        @pl.when(k == 1)
        def _():
            for s in range(1, 8):
                sum_copy(s, lax.rem(c + s, 8)).wait_recv()
            spread_start()

        @pl.when(k == 2)
        def _():
            spread_relay()

        @pl.when(k == 3)
        def _():
            spread_relay_far()

        low = FIRST_STEPS + STEPS_PER_BLOCK * k
        bulk(low, jnp.where(k == 3, 9, jnp.minimum(low + STEPS_PER_BLOCK, 9)))

    spread_copy(1 - core, c_s, sibling).wait_recv()
    spread_end()
    for s in range(1, 8):
        sum_copy(s, c).wait_send()
    substitute(A, inverses, X)

    @pl.when(c != 0)
    def _():
        @pl.loop(1, 8)
        def _(s):
            source = lax.rem(c + s, 8)
            for copy in bulk_copy(source, source):
                copy.wait_recv()
            for r in range(4):
                part = pl.ds(r * 128, 128)
                acc[part, :] = acc[part, :] + decode(
                    recvq[source, part, :], rsc[source, pl.ds(r * 4, 4), :], 32
                )

        @pl.loop(0, 4)
        def _(r):
            part = block(r)
            change = tdot(X[:, block(8 + r)], X[:, :1024])
            place = lax.broadcasted_iota(jnp.int32, (128, 1024), 1)
            gone = (place < LEAD) & (b < 2)
            out_ref[part, :] = jnp.where(gone, 0.0, acc[part, :] - change)

    @pl.when(c == 0)
    def _():
        out_ref[...] = X[:, :1024]

    to_x.wait_send()
    for copy in to_z(b, 0) + to_z(x_peer, 1):
        copy.wait_send()

    @pl.loop(0, 8)
    def _(a):
        to_sibling(2 * a + core).wait_send()

    for s in range(1, 8):
        for copy in panel_copy(s, c):
            copy.wait_send()

        a = lax.rem(c + s, 8)

        @pl.when(a != 0)
        def _():
            for copy in bulk_copy(a, c):
                copy.wait_send()

        pivot_copy(s, c).wait_send()
        pivot_sum_copy(s, c).wait_send()

    pivot_half_copy(core).wait_send()


def shards(vectors, primal, dual_inverse, touches):
    dma = pltpu.SemaphoreType.DMA
    vmem = pltpu.VMEM
    anywhere = pl.BlockSpec(memory_space=pl.ANY)
    return pl.pallas_call(
        kernel,
        out_shape=jax.ShapeDtypeStruct((PANEL, 1024), F32),
        in_specs=[pl.BlockSpec(memory_space=pltpu.SMEM), anywhere, anywhere, anywhere],
        out_specs=pl.BlockSpec(memory_space=pltpu.VMEM),
        scratch_shapes=[
            vmem((4096, 1024), BF16),
            vmem((1024, 1024), BF16),
            vmem((1024, 1024), BF16),
            vmem((1024, 1024), BF16),
            vmem((PANEL, 1024), BF16),
            vmem((PANEL, 1024), BF16),
            vmem((8, PANEL, 1024), jnp.int16),
            vmem((8, PANEL, 1024), jnp.int16),
            vmem((8, 16, 1024), F32),
            vmem((8, 16, 1024), F32),
            vmem((PANEL, 1024), F32),
            vmem((64, 1024), F32),
            vmem((8, 64, 1024), jnp.int16),
            vmem((8, 8, 1024), F32),
            vmem((LEAD, PANEL), F32),
            vmem((8, 32, PANEL), F32),
            vmem((2, LEAD, PANEL), F32),
            vmem((PANEL, PANEL), F32),
            vmem((4, 128, 128), F32),
            vmem((PANEL, 1536), F32),
            vmem((128, 256), F32),
            dma((4,)), dma((16,)), dma, dma((2, 3)), dma((8,)),
            dma((8,)), dma((8,)), dma((8,)), dma((8,)), dma((8,)), dma((8,)),
            dma((8,)), dma((8,)), dma((8,)), dma((8,)),
            dma((2,)), dma, dma((3,)), dma,
            dma((8,)), dma((8,)), dma((8,)), dma((8,)), dma, dma,
        ],
        compiler_params=pltpu.CompilerParams(
            collective_id=0, has_side_effects=True, vmem_limit_bytes=60 << 20
        ),
    )(touches, vectors, primal, dual_inverse)


def solution(mesh):
    in_specs = (
        P("cone", "con", None),
        P("cone", None, None),
        P("cone", None, None),
        P("cone", None),
    )
    out_specs = P("cone", "con")
    return jax.shard_map(shards, mesh=mesh, in_specs=in_specs, out_specs=out_specs, check_vma=False)
```

```python
import jax
import jax.numpy as jnp
from jax import lax
from jax.experimental import pallas as pl
from jax.experimental.pallas import tpu as pltpu
from jax.sharding import PartitionSpec as P

PANEL = 512
LEAD = 256
HI = lax.Precision.HIGHEST
F32 = jnp.float32
BF16 = jnp.bfloat16
MESH = pl.DeviceIdType.MESH
OFFSETS = ((0, 1), (0, 3), (1, 0), (0, 2), (1, 1), (1, 3), (1, 2), (0, 0))
PART = 128
HALF_ROWS = 2048


def tdot(a, b):
    return lax.dot_general(
        a, b, (((0,), (0,)), ((), ())), precision=HI, preferred_element_type=F32
    )


def hdot(a, b):
    return lax.dot_general(
        a, b, (((1,), (0,)), ((), ())), precision=HI, preferred_element_type=F32
    )


def micro(block, first):
    d = {}
    for j in range(8):
        column = jnp.broadcast_to(block[:, first + j : first + j + 1], (8, 128))
        for i in range(j, 8):
            d[i, j] = jnp.broadcast_to(column[i : i + 1, :], (8, 128))
    rows = [
        [jnp.broadcast_to(block[i : i + 1, h * 128 : (h + 1) * 128], (8, 128)) for h in range(2)]
        for i in range(8)
    ]
    for j in range(8):
        inverse = lax.rsqrt(d[j, j])
        low = {i: d[i, j] * inverse for i in range(j + 1, 8)}
        rows[j] = [x * inverse for x in rows[j]]
        for k in range(j + 1, 8):
            for i in range(k, 8):
                d[i, k] = d[i, k] - low[i] * low[k]
        for i in range(j + 1, 8):
            rows[i] = [x - low[i] * y for x, y in zip(rows[i], rows[j])]
    place = lax.broadcasted_iota(jnp.int32, (8, 128), 0)
    halves = []
    for h in range(2):
        upper = rows[0][h]
        for i in range(1, 8):
            upper = jnp.where(place == i, rows[i][h], upper)
        halves.append(upper)
    return jnp.concatenate(halves, axis=1)


def diagonal_factor(work):
    for p in range(16):
        upper = micro(work[8 * p : 8 * p + 8, :], 8 * p)
        work[8 * p : 8 * p + 8, :] = upper
        low = 8 * (p + 1)
        if p < 15:
            change = tdot(upper[:, :128], upper)
            work[low:, :] = work[low:, :] - change[low:, :]


def block(i):
    return pl.ds(pl.multiple_of(i * 128, 128), 128)


def factor_step(k, A, inverses, work):
    square = (128, 128)
    eye = lax.broadcasted_iota(jnp.int32, square, 0) == lax.broadcasted_iota(jnp.int32, square, 1)
    here = block(k)
    work[:, :128] = A[here, here]
    work[:, 128:] = eye.astype(F32)
    diagonal_factor(work)
    inverses[k] = work[:, 128:]
    A[here, :] = hdot(work[:, 128:], A[here, :])

    @pl.loop(k + 1, 4)
    def _(r):
        A[block(r), :] = A[block(r), :] - tdot(A[here, block(r)], A[here, :])


def substitute(A, inverses, X):
    @pl.loop(0, 4)
    def _(k):
        here = block(k)
        X[here, :] = hdot(inverses[k], X[here, :])

        @pl.loop(k + 1, 4)
        def _(r):
            X[block(r), :] = X[block(r), :] - tdot(A[here, block(r)], X[here, :])


def encode(h, chunk):
    rows, columns = h.shape
    cut = h.reshape(rows // chunk, chunk, columns)
    peak = jnp.max(jnp.abs(cut), axis=1)
    inverse = jnp.where(peak > 1e-33, 32767.0 / jnp.maximum(peak, 1e-33), 0.0)
    coded = jnp.round(cut * inverse[:, None, :]).astype(jnp.int16)
    return coded.reshape(rows, columns), peak * (1.0 / 32767.0)


def decode(coded, scale, chunk):
    rows, columns = coded.shape
    cut = coded.astype(F32).reshape(rows // chunk, chunk, columns)
    return (cut * scale[:, None, :]).reshape(rows, columns)


def kernel(
    t_ref, v_hbm, p_hbm, d_hbm, out_ref,
    rows, V, Pm, Dm, rp, rd, sendq, recvq, ssc, rsc, acc, psc, pqr, pscr,
    agq, ags, bpart, brecv, bfull, A, inverses, X, work,
    load_sem, g_recv, g_x, g_z, g_s, pr_send, prs_send, pr_recv, prs_recv, ag_send, ag_recv,
    bq_send, bs_send, bq_recv, bs_recv, c_recv, c_x, c_z, c_s,
    br_send, br_recv, ba_send, ba_recv, bx_send, bx_recv, ags_send, ags_recv,
):
    c = lax.axis_index("cone")
    b = lax.axis_index("con")
    z = b // 4
    xh = (b // 2) % 2
    core = b % 2
    x_peer = b + 2 - 4 * xh
    sibling = b + 1 - 2 * core
    z_peers = [lax.rem(b + 4 * k, 16) for k in (1, 2, 3)]

    leads = [
        pltpu.make_async_copy(
            v_hbm.at[0, pl.ds(PART * h, PART), :],
            rows.at[pl.ds(HALF_ROWS * h + PART * b, PART), :],
            load_sem.at[3 + h],
        )
        for h in range(2)
    ]
    loads = [
        pltpu.make_async_copy(h.at[0], m, load_sem.at[k])
        for k, (h, m) in enumerate(((p_hbm, Pm), (d_hbm, Dm), (v_hbm, V)))
    ]
    for load in leads + loads:
        load.start()

    barrier = pltpu.get_barrier_semaphore()
    for peer in [x_peer, sibling] + z_peers:
        pl.semaphore_signal(barrier, inc=1, device_id={"con": peer}, device_id_type=MESH)
    for s in range(1, 8):
        pl.semaphore_signal(
            barrier, inc=1, device_id={"cone": lax.rem(c + s, 8)}, device_id_type=MESH
        )
    pl.semaphore_wait(barrier, 12)

    def block_copy(slot, h, sem, peer):
        ref = rows.at[pl.ds(pl.multiple_of(HALF_ROWS * h + PART * slot, PART), PART), :]
        return pltpu.make_async_remote_copy(
            src_ref=ref, dst_ref=ref, send_sem=sem, recv_sem=g_recv.at[h, slot],
            device_id={"con": peer}, device_id_type=MESH,
        )

    def to_x(h):
        return block_copy(b, h, g_x.at[h], x_peer)

    def to_sibling(slot, h):
        return block_copy(slot, h, g_s.at[h, slot // 2], sibling)

    def to_z(slot, h, which):
        return [block_copy(slot, h, g_z.at[h, which, k], z_peers[k]) for k in range(3)]

    def send_on(slot, h, which):
        for copy in to_z(slot, h, which):
            copy.start()
        to_sibling(slot, h).start()

    def take_x(h):
        block_copy(x_peer, h, g_x.at[h], x_peer).wait_recv()
        send_on(x_peer, h, 1)

    def arrive(a, h):
        @pl.when(a // 2 != z)
        def _():
            slot = 2 * a + core
            block_copy(slot, h, g_x.at[h], x_peer).wait_recv()
            to_sibling(slot, h).start()

    def arrive_sibling(a, h):
        block_copy(2 * a + 1 - core, h, g_x.at[h], x_peer).wait_recv()

    own_flag = t_ref[0, b].astype(F32)

    own_chip = b // 2
    contract = (((1,), (1,)), ((), ()))

    def products(a, h, low, high):
        here = pl.ds(pl.multiple_of(HALF_ROWS * h + LEAD * a, LEAD), LEAD)

        @pl.loop(0, 4)
        def _(n):
            cs = pl.ds(pl.multiple_of(n * 256, 256), 256)
            for matrix, result in ((Pm, rp), (Dm, rd)):
                value = jnp.dot(rows[here, :], matrix[:, cs], preferred_element_type=F32)
                result[low : low + PART, cs] = value[:PART].astype(BF16)
                result[high : high + PART, cs] = value[PART:].astype(BF16)

    def grams(a, count, sink):
        first = t_ref[0, 2 * a].astype(F32) * own_flag
        second = t_ref[0, 2 * a + 1].astype(F32) * own_flag
        place = lax.broadcasted_iota(jnp.int32, (count, 256), 0)
        flags = jnp.where(place < count // 2, first, second)

        @pl.loop(0, 4)
        def _(n):
            cs = pl.ds(pl.multiple_of(n * 256, 256), 256)
            gp = lax.dot_general(rp[:count, :], V[cs, :], contract, preferred_element_type=F32)
            gd = lax.dot_general(rd[:count, :], V[cs, :], contract, preferred_element_type=F32)
            sink(cs, gp * gd * flags)

    def piece(i, size):
        return pl.ds(pl.multiple_of(i * size, size), size)

    def pivot_part():
        half = piece(core, LEAD)
        row_flag = t_ref[0, core].astype(F32)
        place = lax.broadcasted_iota(jnp.int32, (LEAD, PANEL), 1)
        flags = jnp.where(place < LEAD, t_ref[0, 0].astype(F32), t_ref[0, 1].astype(F32)) * row_flag
        lead_rows = jnp.concatenate(
            [rows[HALF_ROWS * h + PART * k : HALF_ROWS * h + PART * (k + 1), :]
             for k in range(2) for h in range(2)],
            axis=0,
        )
        gp = lax.dot_general(rp[half, :], lead_rows, contract, preferred_element_type=F32)
        gd = lax.dot_general(rd[half, :], lead_rows, contract, preferred_element_type=F32)
        bpart[...] = gp * gd * flags

    def pivot_copy(s, slot):
        peer = lax.rem(c + s, 8)
        return pltpu.make_async_remote_copy(
            src_ref=bpart.at[piece(peer, 32), :], dst_ref=brecv.at[slot],
            send_sem=br_send.at[s], recv_sem=br_recv.at[slot],
            device_id={"cone": peer}, device_id_type=MESH,
        )

    def pivot_sum_copy(s, slot):
        ref = bfull.at[core, piece(slot, 32), :]
        return pltpu.make_async_remote_copy(
            src_ref=ref, dst_ref=ref, send_sem=ba_send.at[s], recv_sem=ba_recv.at[slot],
            device_id={"cone": lax.rem(c + s, 8)}, device_id_type=MESH,
        )

    def pivot_half_copy(half):
        ref = bfull.at[half]
        return pltpu.make_async_remote_copy(
            src_ref=ref, dst_ref=ref, send_sem=bx_send, recv_sem=bx_recv,
            device_id={"con": sibling}, device_id_type=MESH,
        )

    def panel_sink(cs, h):
        X[:, cs] = h
        coded, scale = encode(h, 8)
        sendq[0, :, cs] = coded
        psc[:, cs] = scale

    def panel_copy(s, slot):
        peer = lax.rem(c + s, 8)
        return (
            pltpu.make_async_remote_copy(
                src_ref=sendq.at[0, piece(peer, 64), :], dst_ref=pqr.at[slot],
                send_sem=pr_send.at[s], recv_sem=pr_recv.at[slot],
                device_id={"cone": peer}, device_id_type=MESH,
            ),
            pltpu.make_async_remote_copy(
                src_ref=psc.at[piece(peer, 8), :], dst_ref=pscr.at[slot],
                send_sem=prs_send.at[s], recv_sem=prs_recv.at[slot],
                device_id={"cone": peer}, device_id_type=MESH,
            ),
        )

    def sum_copy(s, slot):
        peer = lax.rem(c + s, 8)
        return (
            pltpu.make_async_remote_copy(
                src_ref=agq.at[slot], dst_ref=agq.at[slot],
                send_sem=ag_send.at[s], recv_sem=ag_recv.at[slot],
                device_id={"cone": peer}, device_id_type=MESH,
            ),
            pltpu.make_async_remote_copy(
                src_ref=ags.at[slot], dst_ref=ags.at[slot],
                send_sem=ags_send.at[s], recv_sem=ags_recv.at[slot],
                device_id={"cone": peer}, device_id_type=MESH,
            ),
        )

    def bulk_copy(a, slot, h, part=None):
        here = piece(h, LEAD) if part is None else piece(2 * h + part, PART)
        scales = piece(h, 8)
        return (
            pltpu.make_async_remote_copy(
                src_ref=sendq.at[a, here, :], dst_ref=recvq.at[slot, here, :],
                send_sem=bq_send.at[h, a], recv_sem=bq_recv.at[h, slot],
                device_id={"cone": a}, device_id_type=MESH,
            ),
            pltpu.make_async_remote_copy(
                src_ref=ssc.at[a, scales, :], dst_ref=rsc.at[slot, scales, :],
                send_sem=bs_send.at[h, a], recv_sem=bs_recv.at[h, slot],
                device_id={"cone": a}, device_id_type=MESH,
            ),
        )

    def compute(a, h):
        here = piece(h, LEAD)

        def sink(cs, value):
            @pl.when(a == c)
            def _():
                acc[here, cs] = value

            @pl.when(a != c)
            def _():
                coded, scale = encode(value, 32)
                sendq[a, here, cs] = coded
                ssc[a, piece(h, 8), cs] = scale

        arrive_sibling(a, h)
        products(a, h, 0, PART)
        grams(a, LEAD, sink)

    def target(t):
        dx = dy = 0
        for k, (x, y) in enumerate(OFFSETS):
            dx = jnp.where(t == k + 1, x, dx)
            dy = jnp.where(t == k + 1, y, dy)
        return lax.rem(c // 4 + dx, 2) * 4 + lax.rem(lax.rem(c, 4) + dy, 4)

    def issue(low, high, h):
        for part in range(2):
            for t in range(low, high):
                a = target(t)

                @pl.when(a != 0)
                def _():
                    coded, scale = bulk_copy(a, c, h, part)
                    if part == 0:
                        scale.start()
                    coded.start()

    def bulk(low, high, h):
        @pl.loop(low, high)
        def _(t):
            a = target(t)

            @pl.when(a != 0)
            def _():
                compute(a, h)

            @pl.when(t == 3)
            def _():
                issue(1, 4, h)

            @pl.when(t == 7)
            def _():
                issue(4, 8, h)

    def arrive_all(h):
        @pl.loop(1, 8)
        def _(a):
            arrive(a, h)

    def accumulate(h):
        @pl.loop(1, 8)
        def _(s):
            source = lax.rem(c + s, 8)
            for copy in bulk_copy(source, source, h):
                copy.wait_recv()
            for r in range(2):
                part = piece(2 * h + r, PART)
                scales = rsc[source, piece(h, 8), :]
                acc[part, :] = acc[part, :] + decode(
                    recvq[source, part, :], scales[4 * r : 4 * r + 4], 32
                )

    def spread_copy(slot, sem, peer):
        ref = X.at[:, pl.ds(pl.multiple_of(1024 + slot * LEAD, LEAD), LEAD)]
        return pltpu.make_async_remote_copy(
            src_ref=ref, dst_ref=ref, send_sem=sem, recv_sem=c_recv.at[slot],
            device_id={"con": peer}, device_id_type=MESH,
        )

    at_home_z = z == c // 2
    at_home_x = xh == lax.rem(c, 2)

    def spread_on():
        for k in range(3):
            spread_copy(core, c_z.at[k], z_peers[k]).start()
        spread_copy(core, c_s, sibling).start()

    def spread_start():
        @pl.when(at_home_z & at_home_x)
        def _():
            X[:, pl.ds(pl.multiple_of(1024 + core * LEAD, LEAD), LEAD)] = X[:, :LEAD]
            spread_copy(core, c_x, x_peer).start()
            spread_on()

    def spread_relay():
        @pl.when(at_home_z & (xh != lax.rem(c, 2)))
        def _():
            spread_copy(core, c_x, x_peer).wait_recv()
            spread_on()

    def spread_relay_far():
        @pl.when(z != c // 2)
        def _():
            spread_copy(core, c_x, x_peer).wait_recv()
            spread_copy(core, c_s, sibling).start()

    def spread_end():
        spread_copy(core, c_s, sibling).wait_send()

        @pl.when(at_home_z)
        def _():
            for k in range(3):
                spread_copy(core, c_z.at[k], z_peers[k]).wait_send()

        @pl.when(at_home_z & at_home_x)
        def _():
            spread_copy(core, c_x, x_peer).wait_send()

    for lead in leads:
        lead.wait()
    for h in range(2):
        to_x(h).start()
    send_on(b, 0, 0)

    @pl.when(own_chip == 0)
    def _():
        send_on(b, 1, 0)

    for load in loads:
        load.wait()
    take_x(0)

    @pl.when(x_peer // 2 == 0)
    def _():
        take_x(1)

    for h in range(2):
        arrive(0, h)
    for h in range(2):
        arrive_sibling(0, h)
        products(0, h, PART * h, LEAD + PART * h)
    pivot_part()
    for s in range(1, 8):
        pivot_copy(s, c).start()

    grams(0, PANEL, panel_sink)
    arrive_all(0)

    @pl.when(own_chip != 0)
    def _():
        send_on(b, 1, 0)

    @pl.when(x_peer // 2 != 0)
    def _():
        take_x(1)

    half_piece = piece(c, 32)
    bfull[core, half_piece, :] = bpart[half_piece, :]

    @pl.loop(1, 8)
    def _(s):
        source = lax.rem(c + s, 8)
        pivot_copy(s, source).wait_recv()
        bfull[core, half_piece, :] = bfull[core, half_piece, :] + brecv[source]

    for s in range(1, 8):
        pivot_sum_copy(s, c).start()
    for s in range(1, 8):
        for copy in panel_copy(s, c):
            copy.start()

    bulk(1, 4, 0)

    for s in range(1, 8):
        pivot_sum_copy(s, lax.rem(c + s, 8)).wait_recv()
    pivot_half_copy(core).start()

    mine = piece(c, 64)

    @pl.loop(1, 8)
    def _(s):
        source = lax.rem(c + s, 8)
        for copy in panel_copy(s, source):
            copy.wait_recv()
        X[mine, :1024] = X[mine, :1024] + decode(pqr[source], pscr[source], 8)

    agq[c], ags[c] = encode(X[mine, :1024], 8)
    for s in range(1, 8):
        for copy in sum_copy(s, c):
            copy.start()

    bulk(4, 9, 0)
    arrive_all(1)

    pivot_half_copy(1 - core).wait_recv()
    A[:LEAD, :] = bfull[0]
    A[LEAD:, :] = bfull[1]
    A[...] = (A[...] + A[...].T) * 0.5

    @pl.loop(0, 4)
    def _(k):
        low = jnp.where(k == 0, 1, jnp.where(k == 1, 4, 9))
        high = jnp.where(k == 0, 4, 9)
        bulk(low, high, 1)
        factor_step(k, A, inverses, work)

        @pl.when(k == 1)
        def _():
            for s in range(1, 8):
                for copy in sum_copy(s, lax.rem(c + s, 8)):
                    copy.wait_recv()

            @pl.loop(0, 8)
            def _(s):
                X[piece(s, 64), :1024] = decode(agq[s], ags[s], 8)

            spread_start()

        @pl.when(k == 2)
        def _():
            spread_relay()

        @pl.when(k == 3)
        def _():
            spread_relay_far()

    @pl.when(c != 0)
    def _():
        accumulate(0)

    spread_copy(1 - core, c_s, sibling).wait_recv()
    spread_end()
    substitute(A, inverses, X)

    @pl.when(c != 0)
    def _():
        accumulate(1)

        @pl.loop(0, 4)
        def _(q):
            r = 2 * (q % 2) + q // 2
            change = tdot(X[:, block(8 + r)], X[:, :1024])
            place = lax.broadcasted_iota(jnp.int32, (128, 1024), 1)
            gone = (place < LEAD) & (b < 2)
            out_ref[block(r), :] = jnp.where(gone, 0.0, acc[block(q), :] - change)

    @pl.when(c == 0)
    def _():
        out_ref[...] = X[:, :1024]

    for h in range(2):
        to_x(h).wait_send()
        for copy in to_z(b, h, 0) + to_z(x_peer, h, 1):
            copy.wait_send()

        @pl.loop(0, 8)
        def _(a):
            to_sibling(2 * a + core, h).wait_send()

    for s in range(1, 8):
        for copy in panel_copy(s, c) + sum_copy(s, c):
            copy.wait_send()

        a = lax.rem(c + s, 8)

        @pl.when(a != 0)
        def _():
            for h in range(2):
                for copy in bulk_copy(a, c, h):
                    copy.wait_send()

        pivot_copy(s, c).wait_send()
        pivot_sum_copy(s, c).wait_send()

    pivot_half_copy(core).wait_send()


def shards(vectors, primal, dual_inverse, touches):
    dma = pltpu.SemaphoreType.DMA
    vmem = pltpu.VMEM
    anywhere = pl.BlockSpec(memory_space=pl.ANY)
    return pl.pallas_call(
        kernel,
        out_shape=jax.ShapeDtypeStruct((PANEL, 1024), F32),
        in_specs=[pl.BlockSpec(memory_space=pltpu.SMEM), anywhere, anywhere, anywhere],
        out_specs=pl.BlockSpec(memory_space=pltpu.VMEM),
        scratch_shapes=[
            vmem((4096, 1024), BF16),
            vmem((1024, 1024), BF16),
            vmem((1024, 1024), BF16),
            vmem((1024, 1024), BF16),
            vmem((PANEL, 1024), BF16),
            vmem((PANEL, 1024), BF16),
            vmem((8, PANEL, 1024), jnp.int16),
            vmem((8, PANEL, 1024), jnp.int16),
            vmem((8, 16, 1024), F32),
            vmem((8, 16, 1024), F32),
            vmem((PANEL, 1024), F32),
            vmem((64, 1024), F32),
            vmem((8, 64, 1024), jnp.int16),
            vmem((8, 8, 1024), F32),
            vmem((8, 64, 1024), jnp.int16),
            vmem((8, 8, 1024), F32),
            vmem((LEAD, PANEL), F32),
            vmem((8, 32, PANEL), F32),
            vmem((2, LEAD, PANEL), F32),
            vmem((PANEL, PANEL), F32),
            vmem((4, 128, 128), F32),
            vmem((PANEL, 1536), F32),
            vmem((128, 256), F32),
            dma((5,)), dma((2, 16)), dma((2,)), dma((2, 2, 3)), dma((2, 8)),
            dma((8,)), dma((8,)), dma((8,)), dma((8,)), dma((8,)), dma((8,)),
            dma((2, 8)), dma((2, 8)), dma((2, 8)), dma((2, 8)),
            dma((2,)), dma, dma((3,)), dma,
            dma((8,)), dma((8,)), dma((8,)), dma((8,)), dma, dma, dma((8,)), dma((8,)),
        ],
        compiler_params=pltpu.CompilerParams(
            collective_id=0, has_side_effects=True, vmem_limit_bytes=60 << 20
        ),
    )(touches, vectors, primal, dual_inverse)


def solution(mesh):
    in_specs = (
        P("cone", "con", None),
        P("cone", None, None),
        P("cone", None, None),
        P("cone", None),
    )
    out_specs = P("cone", "con")
    return jax.shard_map(shards, mesh=mesh, in_specs=in_specs, out_specs=out_specs, check_vma=False)
```

```python
import jax
import jax.numpy as jnp
from jax import lax
from jax.experimental import pallas as pl
from jax.experimental.pallas import tpu as pltpu
from jax.sharding import PartitionSpec as P

PANEL = 512
LEAD = 256
HI = lax.Precision.HIGHEST
F32 = jnp.float32
BF16 = jnp.bfloat16
MESH = pl.DeviceIdType.MESH
OFFSETS = ((0, 1), (0, 3), (1, 0), (0, 2), (1, 1), (1, 3), (1, 2), (0, 0))
PART = 128
HALF_ROWS = 2048


def tdot(a, b):
    return lax.dot_general(
        a, b, (((0,), (0,)), ((), ())), precision=HI, preferred_element_type=F32
    )


def hdot(a, b):
    return lax.dot_general(
        a, b, (((1,), (0,)), ((), ())), precision=HI, preferred_element_type=F32
    )


def micro(block, first):
    d = {}
    for j in range(8):
        column = jnp.broadcast_to(block[:, first + j : first + j + 1], (8, 128))
        for i in range(j, 8):
            d[i, j] = jnp.broadcast_to(column[i : i + 1, :], (8, 128))
    rows = [
        [jnp.broadcast_to(block[i : i + 1, h * 128 : (h + 1) * 128], (8, 128)) for h in range(2)]
        for i in range(8)
    ]
    for j in range(8):
        inverse = lax.rsqrt(d[j, j])
        low = {i: d[i, j] * inverse for i in range(j + 1, 8)}
        rows[j] = [x * inverse for x in rows[j]]
        for k in range(j + 1, 8):
            for i in range(k, 8):
                d[i, k] = d[i, k] - low[i] * low[k]
        for i in range(j + 1, 8):
            rows[i] = [x - low[i] * y for x, y in zip(rows[i], rows[j])]
    place = lax.broadcasted_iota(jnp.int32, (8, 128), 0)
    halves = []
    for h in range(2):
        upper = rows[0][h]
        for i in range(1, 8):
            upper = jnp.where(place == i, rows[i][h], upper)
        halves.append(upper)
    return jnp.concatenate(halves, axis=1)


def diagonal_factor(work):
    for p in range(16):
        upper = micro(work[8 * p : 8 * p + 8, :], 8 * p)
        work[8 * p : 8 * p + 8, :] = upper
        low = 8 * (p + 1)
        if p < 15:
            change = tdot(upper[:, :128], upper)
            work[low:, :] = work[low:, :] - change[low:, :]


def block(i):
    return pl.ds(pl.multiple_of(i * 128, 128), 128)


def factor_step(k, A, inverses, work):
    square = (128, 128)
    eye = lax.broadcasted_iota(jnp.int32, square, 0) == lax.broadcasted_iota(jnp.int32, square, 1)
    here = block(k)
    work[:, :128] = A[here, here]
    work[:, 128:] = eye.astype(F32)
    diagonal_factor(work)
    inverses[k] = work[:, 128:]
    A[here, :] = hdot(work[:, 128:], A[here, :])

    @pl.loop(k + 1, 4)
    def _(r):
        A[block(r), :] = A[block(r), :] - tdot(A[here, block(r)], A[here, :])


def substitute(A, inverses, X):
    @pl.loop(0, 4)
    def _(k):
        here = block(k)
        X[here, :] = hdot(inverses[k], X[here, :])

        @pl.loop(k + 1, 4)
        def _(r):
            X[block(r), :] = X[block(r), :] - tdot(A[here, block(r)], X[here, :])


def encode(h, chunk):
    rows, columns = h.shape
    cut = h.reshape(rows // chunk, chunk, columns)
    peak = jnp.max(jnp.abs(cut), axis=1)
    inverse = jnp.where(peak > 1e-33, 32767.0 / jnp.maximum(peak, 1e-33), 0.0)
    coded = jnp.round(cut * inverse[:, None, :]).astype(jnp.int16)
    return coded.reshape(rows, columns), peak * (1.0 / 32767.0)


def decode(coded, scale, chunk):
    rows, columns = coded.shape
    cut = coded.astype(F32).reshape(rows // chunk, chunk, columns)
    return (cut * scale[:, None, :]).reshape(rows, columns)


def kernel(
    t_ref, v_hbm, p_hbm, d_hbm, out_ref,
    rows, V, Pm, Dm, rp, rd, sendq, recvq, ssc, rsc, acc, psc, pqr, pscr,
    agq, ags, spq, sps, bpart, brecv, bfull, A, inverses, X, work,
    load_sem, g_recv, g_x, g_z, g_s, pr_send, prs_send, pr_recv, prs_recv, ag_send, ag_recv,
    bq_send, bs_send, bq_recv, bs_recv, c_recv, c_send,
    br_send, br_recv, ba_send, ba_recv, bx_send, bx_recv, ags_send, ags_recv,
):
    c = lax.axis_index("cone")
    b = lax.axis_index("con")
    z = b // 4
    xh = (b // 2) % 2
    core = b % 2
    x_peer = b + 2 - 4 * xh
    sibling = b + 1 - 2 * core
    z_peers = [lax.rem(b + 4 * k, 16) for k in (1, 2, 3)]

    leads = [
        pltpu.make_async_copy(
            v_hbm.at[0, pl.ds(PART * h, PART), :],
            rows.at[pl.ds(HALF_ROWS * h + PART * b, PART), :],
            load_sem.at[3 + h],
        )
        for h in range(2)
    ]
    loads = [
        pltpu.make_async_copy(h.at[0], m, load_sem.at[k])
        for k, (h, m) in enumerate(((p_hbm, Pm), (d_hbm, Dm), (v_hbm, V)))
    ]
    for load in leads + loads:
        load.start()

    barrier = pltpu.get_barrier_semaphore()
    for peer in [x_peer, sibling] + z_peers:
        pl.semaphore_signal(barrier, inc=1, device_id={"con": peer}, device_id_type=MESH)
    for s in range(1, 8):
        pl.semaphore_signal(
            barrier, inc=1, device_id={"cone": lax.rem(c + s, 8)}, device_id_type=MESH
        )
    pl.semaphore_wait(barrier, 12)

    def block_copy(slot, h, sem, peer):
        ref = rows.at[pl.ds(pl.multiple_of(HALF_ROWS * h + PART * slot, PART), PART), :]
        return pltpu.make_async_remote_copy(
            src_ref=ref, dst_ref=ref, send_sem=sem, recv_sem=g_recv.at[h, slot],
            device_id={"con": peer}, device_id_type=MESH,
        )

    def to_x(h):
        return block_copy(b, h, g_x.at[h], x_peer)

    def to_sibling(slot, h):
        return block_copy(slot, h, g_s.at[h, slot // 2], sibling)

    def to_z(slot, h, which):
        return [block_copy(slot, h, g_z.at[h, which, k], z_peers[k]) for k in range(3)]

    def send_on(slot, h, which):
        for copy in to_z(slot, h, which):
            copy.start()
        to_sibling(slot, h).start()

    def take_x(h):
        block_copy(x_peer, h, g_x.at[h], x_peer).wait_recv()
        send_on(x_peer, h, 1)

    def arrive(a, h):
        @pl.when(a // 2 != z)
        def _():
            slot = 2 * a + core
            block_copy(slot, h, g_x.at[h], x_peer).wait_recv()
            to_sibling(slot, h).start()

    def arrive_sibling(a, h):
        block_copy(2 * a + 1 - core, h, g_x.at[h], x_peer).wait_recv()

    own_flag = t_ref[0, b].astype(F32)

    own_chip = b // 2
    contract = (((1,), (1,)), ((), ()))

    def products(a, h, low, high):
        here = pl.ds(pl.multiple_of(HALF_ROWS * h + LEAD * a, LEAD), LEAD)

        @pl.loop(0, 4)
        def _(n):
            cs = pl.ds(pl.multiple_of(n * 256, 256), 256)
            for matrix, result in ((Pm, rp), (Dm, rd)):
                value = jnp.dot(rows[here, :], matrix[:, cs], preferred_element_type=F32)
                result[low : low + PART, cs] = value[:PART].astype(BF16)
                result[high : high + PART, cs] = value[PART:].astype(BF16)

    def grams(a, count, sink):
        first = t_ref[0, 2 * a].astype(F32) * own_flag
        second = t_ref[0, 2 * a + 1].astype(F32) * own_flag
        place = lax.broadcasted_iota(jnp.int32, (count, 256), 0)
        flags = jnp.where(place < count // 2, first, second)

        @pl.loop(0, 4)
        def _(n):
            cs = pl.ds(pl.multiple_of(n * 256, 256), 256)
            gp = lax.dot_general(rp[:count, :], V[cs, :], contract, preferred_element_type=F32)
            gd = lax.dot_general(rd[:count, :], V[cs, :], contract, preferred_element_type=F32)
            sink(cs, gp * gd * flags)

    def piece(i, size):
        return pl.ds(pl.multiple_of(i * size, size), size)

    def pivot_part():
        half = piece(core, LEAD)
        row_flag = t_ref[0, core].astype(F32)
        place = lax.broadcasted_iota(jnp.int32, (LEAD, PANEL), 1)
        flags = jnp.where(place < LEAD, t_ref[0, 0].astype(F32), t_ref[0, 1].astype(F32)) * row_flag
        lead_rows = jnp.concatenate(
            [rows[HALF_ROWS * h + PART * k : HALF_ROWS * h + PART * (k + 1), :]
             for k in range(2) for h in range(2)],
            axis=0,
        )
        gp = lax.dot_general(rp[half, :], lead_rows, contract, preferred_element_type=F32)
        gd = lax.dot_general(rd[half, :], lead_rows, contract, preferred_element_type=F32)
        bpart[...] = gp * gd * flags

    def pivot_copy(s, slot):
        peer = lax.rem(c + s, 8)
        return pltpu.make_async_remote_copy(
            src_ref=bpart.at[piece(peer, 32), :], dst_ref=brecv.at[slot],
            send_sem=br_send.at[s], recv_sem=br_recv.at[slot],
            device_id={"cone": peer}, device_id_type=MESH,
        )

    def pivot_sum_copy(s, slot):
        ref = bfull.at[core, piece(slot, 32), :]
        return pltpu.make_async_remote_copy(
            src_ref=ref, dst_ref=ref, send_sem=ba_send.at[s], recv_sem=ba_recv.at[slot],
            device_id={"cone": lax.rem(c + s, 8)}, device_id_type=MESH,
        )

    def pivot_half_copy(half):
        ref = bfull.at[half]
        return pltpu.make_async_remote_copy(
            src_ref=ref, dst_ref=ref, send_sem=bx_send, recv_sem=bx_recv,
            device_id={"con": sibling}, device_id_type=MESH,
        )

    def panel_sink(cs, h):
        X[:, cs] = h
        coded, scale = encode(h, 8)
        sendq[0, :, cs] = coded
        psc[:, cs] = scale

    def panel_copy(s, slot):
        peer = lax.rem(c + s, 8)
        return (
            pltpu.make_async_remote_copy(
                src_ref=sendq.at[0, piece(peer, 64), :], dst_ref=pqr.at[slot],
                send_sem=pr_send.at[s], recv_sem=pr_recv.at[slot],
                device_id={"cone": peer}, device_id_type=MESH,
            ),
            pltpu.make_async_remote_copy(
                src_ref=psc.at[piece(peer, 8), :], dst_ref=pscr.at[slot],
                send_sem=prs_send.at[s], recv_sem=prs_recv.at[slot],
                device_id={"cone": peer}, device_id_type=MESH,
            ),
        )

    def sum_copy(s, slot):
        peer = lax.rem(c + s, 8)
        return (
            pltpu.make_async_remote_copy(
                src_ref=agq.at[slot], dst_ref=agq.at[slot],
                send_sem=ag_send.at[s], recv_sem=ag_recv.at[slot],
                device_id={"cone": peer}, device_id_type=MESH,
            ),
            pltpu.make_async_remote_copy(
                src_ref=ags.at[slot], dst_ref=ags.at[slot],
                send_sem=ags_send.at[s], recv_sem=ags_recv.at[slot],
                device_id={"cone": peer}, device_id_type=MESH,
            ),
        )

    def bulk_copy(a, slot, h, part=None):
        here = piece(h, LEAD) if part is None else piece(2 * h + part, PART)
        scales = piece(h, 8)
        return (
            pltpu.make_async_remote_copy(
                src_ref=sendq.at[a, here, :], dst_ref=recvq.at[slot, here, :],
                send_sem=bq_send.at[h, a], recv_sem=bq_recv.at[h, slot],
                device_id={"cone": a}, device_id_type=MESH,
            ),
            pltpu.make_async_remote_copy(
                src_ref=ssc.at[a, scales, :], dst_ref=rsc.at[slot, scales, :],
                send_sem=bs_send.at[h, a], recv_sem=bs_recv.at[h, slot],
                device_id={"cone": a}, device_id_type=MESH,
            ),
        )

    def compute(a, h):
        here = piece(h, LEAD)

        def sink(cs, value):
            @pl.when(a == c)
            def _():
                acc[here, cs] = value

            @pl.when(a != c)
            def _():
                coded, scale = encode(value, 32)
                sendq[a, here, cs] = coded
                ssc[a, piece(h, 8), cs] = scale

        arrive_sibling(a, h)
        products(a, h, 0, PART)
        grams(a, LEAD, sink)

    def target(t):
        dx = dy = 0
        for k, (x, y) in enumerate(OFFSETS):
            dx = jnp.where(t == k + 1, x, dx)
            dy = jnp.where(t == k + 1, y, dy)
        return lax.rem(c // 4 + dx, 2) * 4 + lax.rem(lax.rem(c, 4) + dy, 4)

    def issue(low, high, h):
        for part in range(2):
            for t in range(low, high):
                a = target(t)

                @pl.when(a != 0)
                def _():
                    coded, scale = bulk_copy(a, c, h, part)
                    if part == 0:
                        scale.start()
                    coded.start()

    def bulk(low, high, h):
        @pl.loop(low, high)
        def _(t):
            a = target(t)

            @pl.when(a != 0)
            def _():
                compute(a, h)

            if h == 1:
                @pl.when(t == 3)
                def _():
                    issue(1, 4, h)

            @pl.when(t == 7)
            def _():
                issue(4, 8, h)

    def arrive_all(h):
        @pl.loop(1, 8)
        def _(a):
            arrive(a, h)

    def accumulate(h):
        @pl.loop(1, 8)
        def _(s):
            source = lax.rem(c + s, 8)
            for copy in bulk_copy(source, source, h):
                copy.wait_recv()
            for r in range(2):
                part = piece(2 * h + r, PART)
                scales = rsc[source, piece(h, 8), :]
                acc[part, :] = acc[part, :] + decode(
                    recvq[source, part, :], scales[4 * r : 4 * r + 4], 32
                )

    def spread_copy(slot, place, peer):
        return [
            pltpu.make_async_remote_copy(
                src_ref=ref.at[slot], dst_ref=ref.at[slot],
                send_sem=c_send.at[kind, place], recv_sem=c_recv.at[kind, slot],
                device_id={"con": peer}, device_id_type=MESH,
            )
            for kind, ref in enumerate((spq, sps))
        ]

    at_home_z = z == c // 2
    at_home_x = xh == lax.rem(c, 2)

    def spread_take(slot):
        for copy in spread_copy(slot, 0, sibling):
            copy.wait_recv()

    def spread_send(place, peer, sent=False):
        for copy in spread_copy(core, place, peer):
            if sent:
                copy.wait_send()
            else:
                copy.start()

    def spread_on():
        for k in range(3):
            spread_send(2 + k, z_peers[k])
        spread_send(0, sibling)

    def spread_start():
        @pl.when(at_home_z & at_home_x)
        def _():
            spq[core] = agq[:, :, :LEAD]
            sps[core] = ags[:, :, :LEAD]
            spread_send(1, x_peer)
            spread_on()

    def spread_relay():
        @pl.when(at_home_z & (xh != lax.rem(c, 2)))
        def _():
            spread_take(core)
            spread_on()

    def spread_relay_far():
        @pl.when(z != c // 2)
        def _():
            spread_take(core)
            spread_send(0, sibling)

    def spread_end():
        spread_send(0, sibling, sent=True)

        @pl.when(at_home_z)
        def _():
            for k in range(3):
                spread_send(2 + k, z_peers[k], sent=True)

        @pl.when(at_home_z & at_home_x)
        def _():
            spread_send(1, x_peer, sent=True)

    for lead in leads:
        lead.wait()
    for h in range(2):
        to_x(h).start()
    send_on(b, 0, 0)

    @pl.when(own_chip == 0)
    def _():
        send_on(b, 1, 0)

    for load in loads:
        load.wait()
    take_x(0)

    @pl.when(x_peer // 2 == 0)
    def _():
        take_x(1)

    for h in range(2):
        arrive(0, h)
    for h in range(2):
        arrive_sibling(0, h)
        products(0, h, PART * h, LEAD + PART * h)
    pivot_part()
    for s in range(1, 8):
        pivot_copy(s, c).start()

    grams(0, PANEL, panel_sink)
    arrive_all(0)

    @pl.when(own_chip != 0)
    def _():
        send_on(b, 1, 0)

    @pl.when(x_peer // 2 != 0)
    def _():
        take_x(1)

    half_piece = piece(c, 32)
    bfull[core, half_piece, :] = bpart[half_piece, :]

    @pl.loop(1, 8)
    def _(s):
        source = lax.rem(c + s, 8)
        pivot_copy(s, source).wait_recv()
        bfull[core, half_piece, :] = bfull[core, half_piece, :] + brecv[source]

    for s in range(1, 8):
        pivot_sum_copy(s, c).start()
    for s in range(1, 8):
        for copy in panel_copy(s, c):
            copy.start()

    bulk(1, 4, 0)

    for s in range(1, 8):
        pivot_sum_copy(s, lax.rem(c + s, 8)).wait_recv()
    pivot_half_copy(core).start()

    mine = piece(c, 64)

    @pl.loop(1, 8)
    def _(s):
        source = lax.rem(c + s, 8)
        for copy in panel_copy(s, source):
            copy.wait_recv()
        X[mine, :1024] = X[mine, :1024] + decode(pqr[source], pscr[source], 8)

    agq[c], ags[c] = encode(X[mine, :1024], 8)
    for s in range(1, 8):
        for copy in sum_copy(s, c):
            copy.start()

    issue(1, 4, 0)
    bulk(4, 9, 0)
    arrive_all(1)

    for s in range(1, 8):
        for copy in sum_copy(s, lax.rem(c + s, 8)):
            copy.wait_recv()
    spread_start()

    @pl.loop(0, 8)
    def _(s):
        X[piece(s, 64), :1024] = decode(agq[s], ags[s], 8)

    pivot_half_copy(1 - core).wait_recv()
    A[:LEAD, :] = bfull[0]
    A[LEAD:, :] = bfull[1]
    A[...] = (A[...] + A[...].T) * 0.5

    @pl.loop(0, 4)
    def _(k):
        low = jnp.where(k == 0, 1, jnp.where(k == 1, 4, 9))
        high = jnp.where(k == 0, 4, 9)
        bulk(low, high, 1)
        factor_step(k, A, inverses, work)

        @pl.when(k == 0)
        def _():
            spread_relay()

        @pl.when(k == 1)
        def _():
            spread_relay_far()

    @pl.when(c != 0)
    def _():
        accumulate(0)

    spread_take(1 - core)

    @pl.loop(0, 8)
    def _(s):
        for slot in range(2):
            low = 1024 + slot * LEAD
            X[piece(s, 64), low : low + LEAD] = decode(spq[slot, s], sps[slot, s], 8)

    substitute(A, inverses, X)

    @pl.when(c != 0)
    def _():
        accumulate(1)

        @pl.loop(0, 4)
        def _(q):
            r = 2 * (q % 2) + q // 2
            change = tdot(X[:, block(8 + r)], X[:, :1024])
            place = lax.broadcasted_iota(jnp.int32, (128, 1024), 1)
            gone = (place < LEAD) & (b < 2)
            out_ref[block(r), :] = jnp.where(gone, 0.0, acc[block(q), :] - change)

    @pl.when(c == 0)
    def _():
        out_ref[...] = X[:, :1024]

    for h in range(2):
        to_x(h).wait_send()
        for copy in to_z(b, h, 0) + to_z(x_peer, h, 1):
            copy.wait_send()

        @pl.loop(0, 8)
        def _(a):
            to_sibling(2 * a + core, h).wait_send()

    for s in range(1, 8):
        for copy in panel_copy(s, c) + sum_copy(s, c):
            copy.wait_send()

        a = lax.rem(c + s, 8)

        @pl.when(a != 0)
        def _():
            for h in range(2):
                for copy in bulk_copy(a, c, h):
                    copy.wait_send()

        pivot_copy(s, c).wait_send()
        pivot_sum_copy(s, c).wait_send()

    pivot_half_copy(core).wait_send()
    spread_end()


def shards(vectors, primal, dual_inverse, touches):
    dma = pltpu.SemaphoreType.DMA
    vmem = pltpu.VMEM
    anywhere = pl.BlockSpec(memory_space=pl.ANY)
    return pl.pallas_call(
        kernel,
        out_shape=jax.ShapeDtypeStruct((PANEL, 1024), F32),
        in_specs=[pl.BlockSpec(memory_space=pltpu.SMEM), anywhere, anywhere, anywhere],
        out_specs=pl.BlockSpec(memory_space=pltpu.VMEM),
        scratch_shapes=[
            vmem((4096, 1024), BF16),
            vmem((1024, 1024), BF16),
            vmem((1024, 1024), BF16),
            vmem((1024, 1024), BF16),
            vmem((PANEL, 1024), BF16),
            vmem((PANEL, 1024), BF16),
            vmem((8, PANEL, 1024), jnp.int16),
            vmem((8, PANEL, 1024), jnp.int16),
            vmem((8, 16, 1024), F32),
            vmem((8, 16, 1024), F32),
            vmem((PANEL, 1024), F32),
            vmem((64, 1024), F32),
            vmem((8, 64, 1024), jnp.int16),
            vmem((8, 8, 1024), F32),
            vmem((8, 64, 1024), jnp.int16),
            vmem((8, 8, 1024), F32),
            vmem((2, 8, 64, LEAD), jnp.int16),
            vmem((2, 8, 8, LEAD), F32),
            vmem((LEAD, PANEL), F32),
            vmem((8, 32, PANEL), F32),
            vmem((2, LEAD, PANEL), F32),
            vmem((PANEL, PANEL), F32),
            vmem((4, 128, 128), F32),
            vmem((PANEL, 1536), F32),
            vmem((128, 256), F32),
            dma((5,)), dma((2, 16)), dma((2,)), dma((2, 2, 3)), dma((2, 8)),
            dma((8,)), dma((8,)), dma((8,)), dma((8,)), dma((8,)), dma((8,)),
            dma((2, 8)), dma((2, 8)), dma((2, 8)), dma((2, 8)),
            dma((2, 2)), dma((2, 5)),
            dma((8,)), dma((8,)), dma((8,)), dma((8,)), dma, dma, dma((8,)), dma((8,)),
        ],
        compiler_params=pltpu.CompilerParams(
            collective_id=0, has_side_effects=True, vmem_limit_bytes=60 << 20
        ),
    )(touches, vectors, primal, dual_inverse)


def solution(mesh):
    in_specs = (
        P("cone", "con", None),
        P("cone", None, None),
        P("cone", None, None),
        P("cone", None),
    )
    out_specs = P("cone", "con")
    return jax.shard_map(shards, mesh=mesh, in_specs=in_specs, out_specs=out_specs, check_vma=False)
```

```python
import jax
import jax.numpy as jnp
from jax import lax
from jax.experimental import pallas as pl
from jax.experimental.pallas import tpu as pltpu
from jax.sharding import PartitionSpec as P

PANEL = 512
LEAD = 256
HI = lax.Precision.HIGHEST
F32 = jnp.float32
BF16 = jnp.bfloat16
MESH = pl.DeviceIdType.MESH
OFFSETS = ((0, 1), (0, 3), (1, 0), (0, 2), (1, 1), (1, 3), (1, 2), (0, 0))
PART = 128
HALF_ROWS = 2048


def tdot(a, b):
    return lax.dot_general(
        a, b, (((0,), (0,)), ((), ())), precision=HI, preferred_element_type=F32
    )


def hdot(a, b):
    return lax.dot_general(
        a, b, (((1,), (0,)), ((), ())), precision=HI, preferred_element_type=F32
    )


def micro(block, first):
    d = {}
    for j in range(8):
        column = jnp.broadcast_to(block[:, first + j : first + j + 1], (8, 128))
        for i in range(j, 8):
            d[i, j] = jnp.broadcast_to(column[i : i + 1, :], (8, 128))
    rows = [
        [jnp.broadcast_to(block[i : i + 1, h * 128 : (h + 1) * 128], (8, 128)) for h in range(2)]
        for i in range(8)
    ]
    for j in range(8):
        inverse = lax.rsqrt(d[j, j])
        low = {i: d[i, j] * inverse for i in range(j + 1, 8)}
        rows[j] = [x * inverse for x in rows[j]]
        for k in range(j + 1, 8):
            for i in range(k, 8):
                d[i, k] = d[i, k] - low[i] * low[k]
        for i in range(j + 1, 8):
            rows[i] = [x - low[i] * y for x, y in zip(rows[i], rows[j])]
    place = lax.broadcasted_iota(jnp.int32, (8, 128), 0)
    halves = []
    for h in range(2):
        upper = rows[0][h]
        for i in range(1, 8):
            upper = jnp.where(place == i, rows[i][h], upper)
        halves.append(upper)
    return jnp.concatenate(halves, axis=1)


def diagonal_factor(work):
    for p in range(16):
        upper = micro(work[8 * p : 8 * p + 8, :], 8 * p)
        work[8 * p : 8 * p + 8, :] = upper
        low = 8 * (p + 1)
        if p < 15:
            change = tdot(upper[:, :128], upper)
            work[low:, :] = work[low:, :] - change[low:, :]


def block(i):
    return pl.ds(pl.multiple_of(i * 128, 128), 128)


def factor_step(k, A, inverses, work):
    square = (128, 128)
    eye = lax.broadcasted_iota(jnp.int32, square, 0) == lax.broadcasted_iota(jnp.int32, square, 1)
    here = block(k)
    work[:, :128] = A[here, here]
    work[:, 128:] = eye.astype(F32)
    diagonal_factor(work)
    inverses[k] = work[:, 128:]
    A[here, :] = hdot(work[:, 128:], A[here, :])

    @pl.loop(k + 1, 4)
    def _(r):
        A[block(r), :] = A[block(r), :] - tdot(A[here, block(r)], A[here, :])


def substitute(A, inverses, X):
    @pl.loop(0, 4)
    def _(k):
        here = block(k)
        X[here, :] = hdot(inverses[k], X[here, :])

        @pl.loop(k + 1, 4)
        def _(r):
            X[block(r), :] = X[block(r), :] - tdot(A[here, block(r)], X[here, :])


def encode(h, chunk):
    rows, columns = h.shape
    cut = h.reshape(rows // chunk, chunk, columns)
    peak = jnp.max(jnp.abs(cut), axis=1)
    inverse = jnp.where(peak > 1e-33, 32767.0 / jnp.maximum(peak, 1e-33), 0.0)
    coded = jnp.round(cut * inverse[:, None, :]).astype(jnp.int16)
    return coded.reshape(rows, columns), peak * (1.0 / 32767.0)


def decode(coded, scale, chunk):
    rows, columns = coded.shape
    cut = coded.astype(F32).reshape(rows // chunk, chunk, columns)
    return (cut * scale[:, None, :]).reshape(rows, columns)


def kernel(
    t_ref, v_hbm, p_hbm, d_hbm, out_ref,
    rows, V, Pm, Dm, rp, rd, sendq, recvq, ssc, rsc, acc, psc, pqr, pscr,
    agq, ags, spq, sps, bpart, brecv, bfull, A, inverses, X, work,
    load_sem, g_recv, g_x, g_z, g_s, pr_send, prs_send, pr_recv, prs_recv, ag_send, ag_recv,
    bq_send, bs_send, bq_recv, bs_recv, c_recv, c_send,
    br_send, br_recv, ba_send, ba_recv, bx_send, bx_recv, ags_send, ags_recv,
):
    c = lax.axis_index("cone")
    b = lax.axis_index("con")
    z = b // 4
    xh = (b // 2) % 2
    core = b % 2
    x_peer = b + 2 - 4 * xh
    sibling = b + 1 - 2 * core
    z_peers = [lax.rem(b + 4 * k, 16) for k in (1, 2, 3)]

    leads = [
        pltpu.make_async_copy(
            v_hbm.at[0, pl.ds(PART * h, PART), :],
            rows.at[pl.ds(HALF_ROWS * h + PART * b, PART), :],
            load_sem.at[3 + h],
        )
        for h in range(2)
    ]
    loads = [
        pltpu.make_async_copy(h.at[0], m, load_sem.at[k])
        for k, (h, m) in enumerate(((p_hbm, Pm), (d_hbm, Dm), (v_hbm, V)))
    ]
    for load in leads + loads:
        load.start()

    barrier = pltpu.get_barrier_semaphore()
    for peer in [x_peer, sibling] + z_peers:
        pl.semaphore_signal(barrier, inc=1, device_id={"con": peer}, device_id_type=MESH)
    for s in range(1, 8):
        pl.semaphore_signal(
            barrier, inc=1, device_id={"cone": lax.rem(c + s, 8)}, device_id_type=MESH
        )
    pl.semaphore_wait(barrier, 12)

    def block_copy(slot, h, sem, peer):
        ref = rows.at[pl.ds(pl.multiple_of(HALF_ROWS * h + PART * slot, PART), PART), :]
        return pltpu.make_async_remote_copy(
            src_ref=ref, dst_ref=ref, send_sem=sem, recv_sem=g_recv.at[h, slot],
            device_id={"con": peer}, device_id_type=MESH,
        )

    def to_x(h):
        return block_copy(b, h, g_x.at[h], x_peer)

    def to_sibling(slot, h):
        return block_copy(slot, h, g_s.at[h, slot // 2], sibling)

    def to_z(slot, h, which):
        return [block_copy(slot, h, g_z.at[h, which, k], z_peers[k]) for k in range(3)]

    def send_on(slot, h, which):
        for copy in to_z(slot, h, which):
            copy.start()
        to_sibling(slot, h).start()

    def take_x(h):
        block_copy(x_peer, h, g_x.at[h], x_peer).wait_recv()
        send_on(x_peer, h, 1)

    def arrive(a, h):
        @pl.when(a // 2 != z)
        def _():
            slot = 2 * a + core
            block_copy(slot, h, g_x.at[h], x_peer).wait_recv()
            to_sibling(slot, h).start()

    def arrive_sibling(a, h):
        block_copy(2 * a + 1 - core, h, g_x.at[h], x_peer).wait_recv()

    own_flag = t_ref[0, b].astype(F32)

    own_chip = b // 2
    contract = (((1,), (1,)), ((), ()))

    def products(a, h, low, high):
        here = pl.ds(pl.multiple_of(HALF_ROWS * h + LEAD * a, LEAD), LEAD)

        @pl.loop(0, 4)
        def _(n):
            cs = pl.ds(pl.multiple_of(n * 256, 256), 256)
            for matrix, result in ((Pm, rp), (Dm, rd)):
                value = jnp.dot(rows[here, :], matrix[:, cs], preferred_element_type=F32)
                result[low : low + PART, cs] = value[:PART].astype(BF16)
                result[high : high + PART, cs] = value[PART:].astype(BF16)

    def grams(a, count, sink):
        first = t_ref[0, 2 * a].astype(F32) * own_flag
        second = t_ref[0, 2 * a + 1].astype(F32) * own_flag
        place = lax.broadcasted_iota(jnp.int32, (count, 256), 0)
        flags = jnp.where(place < count // 2, first, second)

        @pl.loop(0, 4)
        def _(n):
            cs = pl.ds(pl.multiple_of(n * 256, 256), 256)
            gp = lax.dot_general(rp[:count, :], V[cs, :], contract, preferred_element_type=F32)
            gd = lax.dot_general(rd[:count, :], V[cs, :], contract, preferred_element_type=F32)
            sink(cs, gp * gd * flags)

    def piece(i, size):
        return pl.ds(pl.multiple_of(i * size, size), size)

    def pivot_part():
        half = piece(core, LEAD)
        row_flag = t_ref[0, core].astype(F32)
        place = lax.broadcasted_iota(jnp.int32, (LEAD, PANEL), 1)
        flags = jnp.where(place < LEAD, t_ref[0, 0].astype(F32), t_ref[0, 1].astype(F32)) * row_flag
        lead_rows = jnp.concatenate(
            [rows[HALF_ROWS * h + PART * k : HALF_ROWS * h + PART * (k + 1), :]
             for k in range(2) for h in range(2)],
            axis=0,
        )
        gp = lax.dot_general(rp[half, :], lead_rows, contract, preferred_element_type=F32)
        gd = lax.dot_general(rd[half, :], lead_rows, contract, preferred_element_type=F32)
        bpart[...] = gp * gd * flags

    def pivot_copy(s, slot):
        peer = lax.rem(c + s, 8)
        return pltpu.make_async_remote_copy(
            src_ref=bpart.at[piece(peer, 32), :], dst_ref=brecv.at[slot],
            send_sem=br_send.at[s], recv_sem=br_recv.at[slot],
            device_id={"cone": peer}, device_id_type=MESH,
        )

    def pivot_sum_copy(s, slot):
        ref = bfull.at[core, piece(slot, 32), :]
        return pltpu.make_async_remote_copy(
            src_ref=ref, dst_ref=ref, send_sem=ba_send.at[s], recv_sem=ba_recv.at[slot],
            device_id={"cone": lax.rem(c + s, 8)}, device_id_type=MESH,
        )

    def pivot_half_copy(half):
        ref = bfull.at[half]
        return pltpu.make_async_remote_copy(
            src_ref=ref, dst_ref=ref, send_sem=bx_send, recv_sem=bx_recv,
            device_id={"con": sibling}, device_id_type=MESH,
        )

    def panel_sink(cs, h):
        X[:, cs] = h
        coded, scale = encode(h, 8)
        sendq[0, :, cs] = coded
        psc[:, cs] = scale

    def panel_copy(s, slot):
        peer = lax.rem(c + s, 8)
        return (
            pltpu.make_async_remote_copy(
                src_ref=sendq.at[0, piece(peer, 64), :], dst_ref=pqr.at[slot],
                send_sem=pr_send.at[s], recv_sem=pr_recv.at[slot],
                device_id={"cone": peer}, device_id_type=MESH,
            ),
            pltpu.make_async_remote_copy(
                src_ref=psc.at[piece(peer, 8), :], dst_ref=pscr.at[slot],
                send_sem=prs_send.at[s], recv_sem=prs_recv.at[slot],
                device_id={"cone": peer}, device_id_type=MESH,
            ),
        )

    def sum_copy(s, slot):
        peer = lax.rem(c + s, 8)
        return (
            pltpu.make_async_remote_copy(
                src_ref=agq.at[slot], dst_ref=agq.at[slot],
                send_sem=ag_send.at[s], recv_sem=ag_recv.at[slot],
                device_id={"cone": peer}, device_id_type=MESH,
            ),
            pltpu.make_async_remote_copy(
                src_ref=ags.at[slot], dst_ref=ags.at[slot],
                send_sem=ags_send.at[s], recv_sem=ags_recv.at[slot],
                device_id={"cone": peer}, device_id_type=MESH,
            ),
        )

    def bulk_copy(a, slot, h, part=None):
        here = piece(h, LEAD) if part is None else piece(2 * h + part, PART)
        scales = piece(h, 8)
        return (
            pltpu.make_async_remote_copy(
                src_ref=sendq.at[a, here, :], dst_ref=recvq.at[slot, here, :],
                send_sem=bq_send.at[h, a], recv_sem=bq_recv.at[h, slot],
                device_id={"cone": a}, device_id_type=MESH,
            ),
            pltpu.make_async_remote_copy(
                src_ref=ssc.at[a, scales, :], dst_ref=rsc.at[slot, scales, :],
                send_sem=bs_send.at[h, a], recv_sem=bs_recv.at[h, slot],
                device_id={"cone": a}, device_id_type=MESH,
            ),
        )

    def compute(a, h):
        here = piece(h, LEAD)

        def sink(cs, value):
            @pl.when(a == c)
            def _():
                acc[here, cs] = value

            @pl.when(a != c)
            def _():
                coded, scale = encode(value, 32)
                sendq[a, here, cs] = coded
                ssc[a, piece(h, 8), cs] = scale

        arrive_sibling(a, h)
        products(a, h, 0, PART)
        grams(a, LEAD, sink)

    def target(t):
        dx = dy = 0
        for k, (x, y) in enumerate(OFFSETS):
            dx = jnp.where(t == k + 1, x, dx)
            dy = jnp.where(t == k + 1, y, dy)
        return lax.rem(c // 4 + dx, 2) * 4 + lax.rem(lax.rem(c, 4) + dy, 4)

    def issue(low, high, h):
        for part in range(2):
            for t in range(low, high):
                a = target(t)

                @pl.when(a != 0)
                def _():
                    coded, scale = bulk_copy(a, c, h, part)
                    if part == 0:
                        scale.start()
                    coded.start()

    def bulk(low, high, h):
        @pl.loop(low, high)
        def _(t):
            a = target(t)

            @pl.when(a != 0)
            def _():
                compute(a, h)

            if h == 1:
                @pl.when(t == 3)
                def _():
                    issue(1, 4, h)

            if h == 1:
                @pl.when(t == 7)
                def _():
                    issue(4, 8, h)

    def arrive_all(h):
        @pl.loop(1, 8)
        def _(a):
            arrive(a, h)

    def accumulate(h):
        @pl.loop(1, 8)
        def _(s):
            source = lax.rem(c + s, 8)
            for copy in bulk_copy(source, source, h):
                copy.wait_recv()
            for r in range(2):
                part = piece(2 * h + r, PART)
                scales = rsc[source, piece(h, 8), :]
                acc[part, :] = acc[part, :] + decode(
                    recvq[source, part, :], scales[4 * r : 4 * r + 4], 32
                )

    def spread_copy(slot, place, peer):
        return [
            pltpu.make_async_remote_copy(
                src_ref=ref.at[slot], dst_ref=ref.at[slot],
                send_sem=c_send.at[kind, place], recv_sem=c_recv.at[kind, slot],
                device_id={"con": peer}, device_id_type=MESH,
            )
            for kind, ref in enumerate((spq, sps))
        ]

    at_home_z = z == c // 2
    at_home_x = xh == lax.rem(c, 2)

    def spread_take(slot):
        for copy in spread_copy(slot, 0, sibling):
            copy.wait_recv()

    def spread_send(place, peer, sent=False):
        for copy in spread_copy(core, place, peer):
            if sent:
                copy.wait_send()
            else:
                copy.start()

    def spread_on():
        for k in range(3):
            spread_send(2 + k, z_peers[k])
        spread_send(0, sibling)

    def spread_start():
        @pl.when(at_home_z & at_home_x)
        def _():
            spq[core] = agq[:, :, :LEAD]
            sps[core] = ags[:, :, :LEAD]
            spread_send(1, x_peer)
            spread_on()

    def spread_relay():
        @pl.when(at_home_z & (xh != lax.rem(c, 2)))
        def _():
            spread_take(core)
            spread_on()

    def spread_relay_far():
        @pl.when(z != c // 2)
        def _():
            spread_take(core)
            spread_send(0, sibling)

    def spread_end():
        spread_send(0, sibling, sent=True)

        @pl.when(at_home_z)
        def _():
            for k in range(3):
                spread_send(2 + k, z_peers[k], sent=True)

        @pl.when(at_home_z & at_home_x)
        def _():
            spread_send(1, x_peer, sent=True)

    for lead in leads:
        lead.wait()
    for h in range(2):
        to_x(h).start()
    send_on(b, 0, 0)

    @pl.when(own_chip == 0)
    def _():
        send_on(b, 1, 0)

    for load in loads:
        load.wait()
    take_x(0)

    @pl.when(x_peer // 2 == 0)
    def _():
        take_x(1)

    for h in range(2):
        arrive(0, h)
    for h in range(2):
        arrive_sibling(0, h)
        products(0, h, PART * h, LEAD + PART * h)
    pivot_part()
    for s in range(1, 8):
        pivot_copy(s, c).start()

    grams(0, PANEL, panel_sink)
    arrive_all(0)

    @pl.when(own_chip != 0)
    def _():
        send_on(b, 1, 0)

    @pl.when(x_peer // 2 != 0)
    def _():
        take_x(1)

    half_piece = piece(c, 32)
    bfull[core, half_piece, :] = bpart[half_piece, :]

    @pl.loop(1, 8)
    def _(s):
        source = lax.rem(c + s, 8)
        pivot_copy(s, source).wait_recv()
        bfull[core, half_piece, :] = bfull[core, half_piece, :] + brecv[source]

    for s in range(1, 8):
        pivot_sum_copy(s, c).start()
    for s in range(1, 8):
        for copy in panel_copy(s, c):
            copy.start()

    bulk(1, 4, 0)

    for s in range(1, 8):
        pivot_sum_copy(s, lax.rem(c + s, 8)).wait_recv()
    pivot_half_copy(core).start()

    mine = piece(c, 64)

    @pl.loop(1, 8)
    def _(s):
        source = lax.rem(c + s, 8)
        for copy in panel_copy(s, source):
            copy.wait_recv()
        X[mine, :1024] = X[mine, :1024] + decode(pqr[source], pscr[source], 8)

    agq[c], ags[c] = encode(X[mine, :1024], 8)
    for s in range(1, 8):
        for copy in sum_copy(s, c):
            copy.start()

    issue(1, 4, 0)
    bulk(4, 9, 0)
    arrive_all(1)

    for s in range(1, 8):
        for copy in sum_copy(s, lax.rem(c + s, 8)):
            copy.wait_recv()
    spread_start()
    issue(4, 8, 0)

    @pl.loop(0, 8)
    def _(s):
        X[piece(s, 64), :1024] = decode(agq[s], ags[s], 8)

    pivot_half_copy(1 - core).wait_recv()
    A[:LEAD, :] = bfull[0]
    A[LEAD:, :] = bfull[1]
    A[...] = (A[...] + A[...].T) * 0.5

    @pl.loop(0, 4)
    def _(k):
        low = jnp.where(k == 0, 1, jnp.where(k == 1, 4, 9))
        high = jnp.where(k == 0, 4, 9)
        bulk(low, high, 1)
        factor_step(k, A, inverses, work)

        @pl.when(k == 0)
        def _():
            spread_relay()

        @pl.when(k == 1)
        def _():
            spread_relay_far()

    @pl.when(c != 0)
    def _():
        accumulate(0)

    spread_take(1 - core)

    @pl.loop(0, 8)
    def _(s):
        for slot in range(2):
            low = 1024 + slot * LEAD
            X[piece(s, 64), low : low + LEAD] = decode(spq[slot, s], sps[slot, s], 8)

    substitute(A, inverses, X)

    @pl.when(c != 0)
    def _():
        accumulate(1)

        @pl.loop(0, 4)
        def _(q):
            r = 2 * (q % 2) + q // 2
            change = tdot(X[:, block(8 + r)], X[:, :1024])
            place = lax.broadcasted_iota(jnp.int32, (128, 1024), 1)
            gone = (place < LEAD) & (b < 2)
            out_ref[block(r), :] = jnp.where(gone, 0.0, acc[block(q), :] - change)

    @pl.when(c == 0)
    def _():
        out_ref[...] = X[:, :1024]

    for h in range(2):
        to_x(h).wait_send()
        for copy in to_z(b, h, 0) + to_z(x_peer, h, 1):
            copy.wait_send()

        @pl.loop(0, 8)
        def _(a):
            to_sibling(2 * a + core, h).wait_send()

    for s in range(1, 8):
        for copy in panel_copy(s, c) + sum_copy(s, c):
            copy.wait_send()

        a = lax.rem(c + s, 8)

        @pl.when(a != 0)
        def _():
            for h in range(2):
                for copy in bulk_copy(a, c, h):
                    copy.wait_send()

        pivot_copy(s, c).wait_send()
        pivot_sum_copy(s, c).wait_send()

    pivot_half_copy(core).wait_send()
    spread_end()


def shards(vectors, primal, dual_inverse, touches):
    dma = pltpu.SemaphoreType.DMA
    vmem = pltpu.VMEM
    anywhere = pl.BlockSpec(memory_space=pl.ANY)
    return pl.pallas_call(
        kernel,
        out_shape=jax.ShapeDtypeStruct((PANEL, 1024), F32),
        in_specs=[pl.BlockSpec(memory_space=pltpu.SMEM), anywhere, anywhere, anywhere],
        out_specs=pl.BlockSpec(memory_space=pltpu.VMEM),
        scratch_shapes=[
            vmem((4096, 1024), BF16),
            vmem((1024, 1024), BF16),
            vmem((1024, 1024), BF16),
            vmem((1024, 1024), BF16),
            vmem((PANEL, 1024), BF16),
            vmem((PANEL, 1024), BF16),
            vmem((8, PANEL, 1024), jnp.int16),
            vmem((8, PANEL, 1024), jnp.int16),
            vmem((8, 16, 1024), F32),
            vmem((8, 16, 1024), F32),
            vmem((PANEL, 1024), F32),
            vmem((64, 1024), F32),
            vmem((8, 64, 1024), jnp.int16),
            vmem((8, 8, 1024), F32),
            vmem((8, 64, 1024), jnp.int16),
            vmem((8, 8, 1024), F32),
            vmem((2, 8, 64, LEAD), jnp.int16),
            vmem((2, 8, 8, LEAD), F32),
            vmem((LEAD, PANEL), F32),
            vmem((8, 32, PANEL), F32),
            vmem((2, LEAD, PANEL), F32),
            vmem((PANEL, PANEL), F32),
            vmem((4, 128, 128), F32),
            vmem((PANEL, 1536), F32),
            vmem((128, 256), F32),
            dma((5,)), dma((2, 16)), dma((2,)), dma((2, 2, 3)), dma((2, 8)),
            dma((8,)), dma((8,)), dma((8,)), dma((8,)), dma((8,)), dma((8,)),
            dma((2, 8)), dma((2, 8)), dma((2, 8)), dma((2, 8)),
            dma((2, 2)), dma((2, 5)),
            dma((8,)), dma((8,)), dma((8,)), dma((8,)), dma, dma, dma((8,)), dma((8,)),
        ],
        compiler_params=pltpu.CompilerParams(
            collective_id=0, has_side_effects=True, vmem_limit_bytes=60 << 20
        ),
    )(touches, vectors, primal, dual_inverse)


def solution(mesh):
    in_specs = (
        P("cone", "con", None),
        P("cone", None, None),
        P("cone", None, None),
        P("cone", None),
    )
    out_specs = P("cone", "con")
    return jax.shard_map(shards, mesh=mesh, in_specs=in_specs, out_specs=out_specs, check_vma=False)
```

```python
import jax
import jax.numpy as jnp
from jax import lax
from jax.experimental import pallas as pl
from jax.experimental.pallas import tpu as pltpu
from jax.sharding import PartitionSpec as P

PANEL = 512
LEAD = 256
HI = lax.Precision.HIGHEST
F32 = jnp.float32
BF16 = jnp.bfloat16
MESH = pl.DeviceIdType.MESH
OFFSETS = ((0, 1), (0, 3), (1, 0), (0, 2), (1, 1), (1, 3), (1, 2), (0, 0))
PART = 128
HALF_ROWS = 2048


def tdot(a, b):
    return lax.dot_general(
        a, b, (((0,), (0,)), ((), ())), precision=HI, preferred_element_type=F32
    )


def hdot(a, b):
    return lax.dot_general(
        a, b, (((1,), (0,)), ((), ())), precision=HI, preferred_element_type=F32
    )


def micro(block, first):
    d = {}
    for j in range(8):
        column = jnp.broadcast_to(block[:, first + j : first + j + 1], (8, 128))
        for i in range(j, 8):
            d[i, j] = jnp.broadcast_to(column[i : i + 1, :], (8, 128))
    rows = [
        [jnp.broadcast_to(block[i : i + 1, h * 128 : (h + 1) * 128], (8, 128)) for h in range(2)]
        for i in range(8)
    ]
    for j in range(8):
        inverse = lax.rsqrt(d[j, j])
        low = {i: d[i, j] * inverse for i in range(j + 1, 8)}
        rows[j] = [x * inverse for x in rows[j]]
        for k in range(j + 1, 8):
            for i in range(k, 8):
                d[i, k] = d[i, k] - low[i] * low[k]
        for i in range(j + 1, 8):
            rows[i] = [x - low[i] * y for x, y in zip(rows[i], rows[j])]
    place = lax.broadcasted_iota(jnp.int32, (8, 128), 0)
    halves = []
    for h in range(2):
        upper = rows[0][h]
        for i in range(1, 8):
            upper = jnp.where(place == i, rows[i][h], upper)
        halves.append(upper)
    return jnp.concatenate(halves, axis=1)


def diagonal_factor(work):
    for p in range(16):
        upper = micro(work[8 * p : 8 * p + 8, :], 8 * p)
        work[8 * p : 8 * p + 8, :] = upper
        low = 8 * (p + 1)
        if p < 15:
            change = tdot(upper[:, :128], upper)
            work[low:, :] = work[low:, :] - change[low:, :]


def block(i):
    return pl.ds(pl.multiple_of(i * 128, 128), 128)


def factor_step(k, A, inverses, work):
    square = (128, 128)
    eye = lax.broadcasted_iota(jnp.int32, square, 0) == lax.broadcasted_iota(jnp.int32, square, 1)
    here = block(k)
    work[:, :128] = A[here, here]
    work[:, 128:] = eye.astype(F32)
    diagonal_factor(work)
    inverses[k] = work[:, 128:]
    A[here, :] = hdot(work[:, 128:], A[here, :])

    @pl.loop(k + 1, 4)
    def _(r):
        A[block(r), :] = A[block(r), :] - tdot(A[here, block(r)], A[here, :])


def substitute(A, inverses, X):
    @pl.loop(0, 4)
    def _(k):
        here = block(k)
        X[here, :] = hdot(inverses[k], X[here, :])

        @pl.loop(k + 1, 4)
        def _(r):
            X[block(r), :] = X[block(r), :] - tdot(A[here, block(r)], X[here, :])


def encode(h, chunk):
    rows, columns = h.shape
    cut = h.reshape(rows // chunk, chunk, columns)
    peak = jnp.max(jnp.abs(cut), axis=1)
    inverse = jnp.where(peak > 1e-33, 32767.0 / jnp.maximum(peak, 1e-33), 0.0)
    coded = jnp.round(cut * inverse[:, None, :]).astype(jnp.int16)
    return coded.reshape(rows, columns), peak * (1.0 / 32767.0)


def decode(coded, scale, chunk):
    rows, columns = coded.shape
    cut = coded.astype(F32).reshape(rows // chunk, chunk, columns)
    return (cut * scale[:, None, :]).reshape(rows, columns)


def kernel(
    t_ref, v_hbm, p_hbm, d_hbm, out_ref,
    rows, V, Pm, Dm, rp, rd, sendq, recvq, ssc, rsc, acc, psc, pqr, pscr,
    agq, ags, spq, sps, bpart, brecv, bfull, A, inverses, X, work,
    load_sem, g_recv, g_x, g_z, g_s, pr_send, prs_send, pr_recv, prs_recv, ag_send, ag_recv,
    bq_send, bs_send, bq_recv, bs_recv, c_recv, c_send,
    br_send, br_recv, ba_send, ba_recv, bx_send, bx_recv, ags_send, ags_recv,
):
    c = lax.axis_index("cone")
    b = lax.axis_index("con")
    z = b // 4
    xh = (b // 2) % 2
    core = b % 2
    x_peer = b + 2 - 4 * xh
    sibling = b + 1 - 2 * core
    z_peers = [lax.rem(b + 4 * k, 16) for k in (1, 2, 3)]

    leads = [
        pltpu.make_async_copy(
            v_hbm.at[0, pl.ds(PART * h, PART), :],
            rows.at[pl.ds(HALF_ROWS * h + PART * b, PART), :],
            load_sem.at[3 + h],
        )
        for h in range(2)
    ]
    loads = [
        pltpu.make_async_copy(h.at[0], m, load_sem.at[k])
        for k, (h, m) in enumerate(((p_hbm, Pm), (d_hbm, Dm), (v_hbm, V)))
    ]
    for load in leads + loads:
        load.start()

    barrier = pltpu.get_barrier_semaphore()
    for peer in [x_peer, sibling] + z_peers:
        pl.semaphore_signal(barrier, inc=1, device_id={"con": peer}, device_id_type=MESH)
    for s in range(1, 8):
        pl.semaphore_signal(
            barrier, inc=1, device_id={"cone": lax.rem(c + s, 8)}, device_id_type=MESH
        )
    pl.semaphore_wait(barrier, 12)

    def block_copy(slot, h, sem, peer):
        ref = rows.at[pl.ds(pl.multiple_of(HALF_ROWS * h + PART * slot, PART), PART), :]
        return pltpu.make_async_remote_copy(
            src_ref=ref, dst_ref=ref, send_sem=sem, recv_sem=g_recv.at[h, slot],
            device_id={"con": peer}, device_id_type=MESH,
        )

    def to_x(h):
        return block_copy(b, h, g_x.at[h], x_peer)

    def to_sibling(slot, h):
        return block_copy(slot, h, g_s.at[h, slot // 2], sibling)

    def to_z(slot, h, which):
        return [block_copy(slot, h, g_z.at[h, which, k], z_peers[k]) for k in range(3)]

    def send_on(slot, h, which):
        for copy in to_z(slot, h, which):
            copy.start()
        to_sibling(slot, h).start()

    def take_x(h):
        block_copy(x_peer, h, g_x.at[h], x_peer).wait_recv()
        send_on(x_peer, h, 1)

    def arrive(a, h):
        @pl.when(a // 2 != z)
        def _():
            slot = 2 * a + core
            block_copy(slot, h, g_x.at[h], x_peer).wait_recv()
            to_sibling(slot, h).start()

    def arrive_sibling(a, h):
        block_copy(2 * a + 1 - core, h, g_x.at[h], x_peer).wait_recv()

    own_flag = t_ref[0, b].astype(F32)

    own_chip = b // 2
    contract = (((1,), (1,)), ((), ()))

    def products(a, h, low, high):
        here = pl.ds(pl.multiple_of(HALF_ROWS * h + LEAD * a, LEAD), LEAD)

        @pl.loop(0, 4)
        def _(n):
            cs = pl.ds(pl.multiple_of(n * 256, 256), 256)
            for matrix, result in ((Pm, rp), (Dm, rd)):
                value = jnp.dot(rows[here, :], matrix[:, cs], preferred_element_type=F32)
                result[low : low + PART, cs] = value[:PART].astype(BF16)
                result[high : high + PART, cs] = value[PART:].astype(BF16)

    def grams(a, count, sink):
        first = t_ref[0, 2 * a].astype(F32) * own_flag
        second = t_ref[0, 2 * a + 1].astype(F32) * own_flag
        place = lax.broadcasted_iota(jnp.int32, (count, 256), 0)
        flags = jnp.where(place < count // 2, first, second)

        @pl.loop(0, 4)
        def _(n):
            cs = pl.ds(pl.multiple_of(n * 256, 256), 256)
            gp = lax.dot_general(rp[:count, :], V[cs, :], contract, preferred_element_type=F32)
            gd = lax.dot_general(rd[:count, :], V[cs, :], contract, preferred_element_type=F32)
            sink(cs, gp * gd * flags)

    def piece(i, size):
        return pl.ds(pl.multiple_of(i * size, size), size)

    def pivot_part():
        half = piece(core, LEAD)
        row_flag = t_ref[0, core].astype(F32)
        place = lax.broadcasted_iota(jnp.int32, (LEAD, PANEL), 1)
        flags = jnp.where(place < LEAD, t_ref[0, 0].astype(F32), t_ref[0, 1].astype(F32)) * row_flag
        lead_rows = jnp.concatenate(
            [rows[HALF_ROWS * h + PART * k : HALF_ROWS * h + PART * (k + 1), :]
             for k in range(2) for h in range(2)],
            axis=0,
        )
        gp = lax.dot_general(rp[half, :], lead_rows, contract, preferred_element_type=F32)
        gd = lax.dot_general(rd[half, :], lead_rows, contract, preferred_element_type=F32)
        bpart[...] = gp * gd * flags

    def pivot_copy(s, slot):
        peer = lax.rem(c + s, 8)
        return pltpu.make_async_remote_copy(
            src_ref=bpart.at[piece(peer, 32), :], dst_ref=brecv.at[slot],
            send_sem=br_send.at[s], recv_sem=br_recv.at[slot],
            device_id={"cone": peer}, device_id_type=MESH,
        )

    def pivot_sum_copy(s, slot):
        ref = bfull.at[core, piece(slot, 32), :]
        return pltpu.make_async_remote_copy(
            src_ref=ref, dst_ref=ref, send_sem=ba_send.at[s], recv_sem=ba_recv.at[slot],
            device_id={"cone": lax.rem(c + s, 8)}, device_id_type=MESH,
        )

    def pivot_half_copy(half):
        ref = bfull.at[half]
        return pltpu.make_async_remote_copy(
            src_ref=ref, dst_ref=ref, send_sem=bx_send, recv_sem=bx_recv,
            device_id={"con": sibling}, device_id_type=MESH,
        )

    def panel_sink(cs, h):
        X[:, cs] = h
        coded, scale = encode(h, 8)
        sendq[0, :, cs] = coded
        psc[:, cs] = scale

    def panel_copy(s, slot):
        peer = lax.rem(c + s, 8)
        return (
            pltpu.make_async_remote_copy(
                src_ref=sendq.at[0, piece(peer, 64), :], dst_ref=pqr.at[slot],
                send_sem=pr_send.at[s], recv_sem=pr_recv.at[slot],
                device_id={"cone": peer}, device_id_type=MESH,
            ),
            pltpu.make_async_remote_copy(
                src_ref=psc.at[piece(peer, 8), :], dst_ref=pscr.at[slot],
                send_sem=prs_send.at[s], recv_sem=prs_recv.at[slot],
                device_id={"cone": peer}, device_id_type=MESH,
            ),
        )

    def sum_copy(s, slot):
        peer = lax.rem(c + s, 8)
        return (
            pltpu.make_async_remote_copy(
                src_ref=agq.at[slot], dst_ref=agq.at[slot],
                send_sem=ag_send.at[s], recv_sem=ag_recv.at[slot],
                device_id={"cone": peer}, device_id_type=MESH,
            ),
            pltpu.make_async_remote_copy(
                src_ref=ags.at[slot], dst_ref=ags.at[slot],
                send_sem=ags_send.at[s], recv_sem=ags_recv.at[slot],
                device_id={"cone": peer}, device_id_type=MESH,
            ),
        )

    def bulk_copy(a, slot, h, part=None):
        here = piece(h, LEAD) if part is None else piece(2 * h + part, PART)
        scales = piece(h, 8)
        return (
            pltpu.make_async_remote_copy(
                src_ref=sendq.at[a, here, :], dst_ref=recvq.at[slot, here, :],
                send_sem=bq_send.at[h, a], recv_sem=bq_recv.at[h, slot],
                device_id={"cone": a}, device_id_type=MESH,
            ),
            pltpu.make_async_remote_copy(
                src_ref=ssc.at[a, scales, :], dst_ref=rsc.at[slot, scales, :],
                send_sem=bs_send.at[h, a], recv_sem=bs_recv.at[h, slot],
                device_id={"cone": a}, device_id_type=MESH,
            ),
        )

    def compute(a, h):
        here = piece(h, LEAD)

        def sink(cs, value):
            @pl.when(a == c)
            def _():
                acc[here, cs] = value

            @pl.when(a != c)
            def _():
                coded, scale = encode(value, 32)
                sendq[a, here, cs] = coded
                ssc[a, piece(h, 8), cs] = scale

        arrive_sibling(a, h)
        products(a, h, 0, PART)
        grams(a, LEAD, sink)

    def target(t):
        dx = dy = 0
        for k, (x, y) in enumerate(OFFSETS):
            dx = jnp.where(t == k + 1, x, dx)
            dy = jnp.where(t == k + 1, y, dy)
        return lax.rem(c // 4 + dx, 2) * 4 + lax.rem(lax.rem(c, 4) + dy, 4)

    def issue(low, high, h):
        for part in range(2):
            for t in range(low, high):
                a = target(t)

                @pl.when(a != 0)
                def _():
                    coded, scale = bulk_copy(a, c, h, part)
                    if part == 0:
                        scale.start()
                    coded.start()

    def bulk(low, high, h):
        @pl.loop(low, high)
        def _(t):
            a = target(t)

            @pl.when(a != 0)
            def _():
                compute(a, h)

            if h == 1:
                @pl.when(t == 3)
                def _():
                    issue(1, 4, h)

            if h == 1:
                @pl.when(t == 7)
                def _():
                    issue(4, 8, h)

    def arrive_all(h):
        @pl.loop(1, 8)
        def _(a):
            arrive(a, h)

    def accumulate(h):
        @pl.loop(1, 8)
        def _(s):
            source = lax.rem(c + s, 8)
            for copy in bulk_copy(source, source, h):
                copy.wait_recv()
            for r in range(2):
                part = piece(2 * h + r, PART)
                scales = rsc[source, piece(h, 8), :]
                acc[part, :] = acc[part, :] + decode(
                    recvq[source, part, :], scales[4 * r : 4 * r + 4], 32
                )

    def spread_copy(slot, place, peer):
        return [
            pltpu.make_async_remote_copy(
                src_ref=ref.at[slot], dst_ref=ref.at[slot],
                send_sem=c_send.at[kind, place], recv_sem=c_recv.at[kind, slot],
                device_id={"con": peer}, device_id_type=MESH,
            )
            for kind, ref in enumerate((spq, sps))
        ]

    at_home_z = z == c // 2
    at_home_x = xh == lax.rem(c, 2)

    def spread_take(slot):
        for copy in spread_copy(slot, 0, sibling):
            copy.wait_recv()

    def spread_send(place, peer, sent=False):
        for copy in spread_copy(core, place, peer):
            if sent:
                copy.wait_send()
            else:
                copy.start()

    def spread_on():
        for k in range(3):
            spread_send(2 + k, z_peers[k])
        spread_send(0, sibling)

    def spread_start():
        @pl.when(at_home_z & at_home_x)
        def _():
            spq[core] = agq[:, :, :LEAD]
            sps[core] = ags[:, :, :LEAD]
            spread_send(1, x_peer)
            spread_on()

    def spread_relay():
        @pl.when(at_home_z & (xh != lax.rem(c, 2)))
        def _():
            spread_take(core)
            spread_on()

    def spread_relay_far():
        @pl.when(z != c // 2)
        def _():
            spread_take(core)
            spread_send(0, sibling)

    def spread_end():
        spread_send(0, sibling, sent=True)

        @pl.when(at_home_z)
        def _():
            for k in range(3):
                spread_send(2 + k, z_peers[k], sent=True)

        @pl.when(at_home_z & at_home_x)
        def _():
            spread_send(1, x_peer, sent=True)

    for lead in leads:
        lead.wait()
    for h in range(2):
        to_x(h).start()
    send_on(b, 0, 0)

    @pl.when(own_chip == 0)
    def _():
        send_on(b, 1, 0)

    for load in loads:
        load.wait()
    take_x(0)

    @pl.when(x_peer // 2 == 0)
    def _():
        take_x(1)

    for h in range(2):
        arrive(0, h)
    for h in range(2):
        arrive_sibling(0, h)
        products(0, h, PART * h, LEAD + PART * h)
    pivot_part()
    for s in range(1, 8):
        pivot_copy(s, c).start()

    grams(0, PANEL, panel_sink)
    arrive_all(0)

    @pl.when(own_chip != 0)
    def _():
        send_on(b, 1, 0)

    @pl.when(x_peer // 2 != 0)
    def _():
        take_x(1)

    half_piece = piece(c, 32)
    bfull[core, half_piece, :] = bpart[half_piece, :]

    @pl.loop(1, 8)
    def _(s):
        source = lax.rem(c + s, 8)
        pivot_copy(s, source).wait_recv()
        bfull[core, half_piece, :] = bfull[core, half_piece, :] + brecv[source]

    for s in range(1, 8):
        pivot_sum_copy(s, c).start()
    for s in range(1, 8):
        for copy in panel_copy(s, c):
            copy.start()

    bulk(1, 4, 0)

    for s in range(1, 8):
        pivot_sum_copy(s, lax.rem(c + s, 8)).wait_recv()
    pivot_half_copy(core).start()

    mine = piece(c, 64)

    @pl.loop(1, 8)
    def _(s):
        source = lax.rem(c + s, 8)
        for copy in panel_copy(s, source):
            copy.wait_recv()
        X[mine, :1024] = X[mine, :1024] + decode(pqr[source], pscr[source], 8)

    agq[c], ags[c] = encode(X[mine, :1024], 8)
    for s in range(1, 8):
        for copy in sum_copy(s, c):
            copy.start()

    bulk(4, 9, 0)
    arrive_all(1)

    for s in range(1, 8):
        for copy in sum_copy(s, lax.rem(c + s, 8)):
            copy.wait_recv()
    spread_start()
    issue(1, 8, 0)

    @pl.loop(0, 8)
    def _(s):
        X[piece(s, 64), :1024] = decode(agq[s], ags[s], 8)

    pivot_half_copy(1 - core).wait_recv()
    A[:LEAD, :] = bfull[0]
    A[LEAD:, :] = bfull[1]
    A[...] = (A[...] + A[...].T) * 0.5

    @pl.loop(0, 4)
    def _(k):
        low = jnp.where(k == 0, 1, jnp.where(k == 1, 4, 9))
        high = jnp.where(k == 0, 4, 9)
        bulk(low, high, 1)
        factor_step(k, A, inverses, work)

        @pl.when(k == 0)
        def _():
            spread_relay()

        @pl.when(k == 1)
        def _():
            spread_relay_far()

    @pl.when(c != 0)
    def _():
        accumulate(0)

    spread_take(1 - core)

    @pl.loop(0, 8)
    def _(s):
        for slot in range(2):
            low = 1024 + slot * LEAD
            X[piece(s, 64), low : low + LEAD] = decode(spq[slot, s], sps[slot, s], 8)

    substitute(A, inverses, X)

    @pl.when(c != 0)
    def _():
        accumulate(1)

        @pl.loop(0, 4)
        def _(q):
            r = 2 * (q % 2) + q // 2
            change = tdot(X[:, block(8 + r)], X[:, :1024])
            place = lax.broadcasted_iota(jnp.int32, (128, 1024), 1)
            gone = (place < LEAD) & (b < 2)
            out_ref[block(r), :] = jnp.where(gone, 0.0, acc[block(q), :] - change)

    @pl.when(c == 0)
    def _():
        out_ref[...] = X[:, :1024]

    for h in range(2):
        to_x(h).wait_send()
        for copy in to_z(b, h, 0) + to_z(x_peer, h, 1):
            copy.wait_send()

        @pl.loop(0, 8)
        def _(a):
            to_sibling(2 * a + core, h).wait_send()

    for s in range(1, 8):
        for copy in panel_copy(s, c) + sum_copy(s, c):
            copy.wait_send()

        a = lax.rem(c + s, 8)

        @pl.when(a != 0)
        def _():
            for h in range(2):
                for copy in bulk_copy(a, c, h):
                    copy.wait_send()

        pivot_copy(s, c).wait_send()
        pivot_sum_copy(s, c).wait_send()

    pivot_half_copy(core).wait_send()
    spread_end()


def shards(vectors, primal, dual_inverse, touches):
    dma = pltpu.SemaphoreType.DMA
    vmem = pltpu.VMEM
    anywhere = pl.BlockSpec(memory_space=pl.ANY)
    return pl.pallas_call(
        kernel,
        out_shape=jax.ShapeDtypeStruct((PANEL, 1024), F32),
        in_specs=[pl.BlockSpec(memory_space=pltpu.SMEM), anywhere, anywhere, anywhere],
        out_specs=pl.BlockSpec(memory_space=pltpu.VMEM),
        scratch_shapes=[
            vmem((4096, 1024), BF16),
            vmem((1024, 1024), BF16),
            vmem((1024, 1024), BF16),
            vmem((1024, 1024), BF16),
            vmem((PANEL, 1024), BF16),
            vmem((PANEL, 1024), BF16),
            vmem((8, PANEL, 1024), jnp.int16),
            vmem((8, PANEL, 1024), jnp.int16),
            vmem((8, 16, 1024), F32),
            vmem((8, 16, 1024), F32),
            vmem((PANEL, 1024), F32),
            vmem((64, 1024), F32),
            vmem((8, 64, 1024), jnp.int16),
            vmem((8, 8, 1024), F32),
            vmem((8, 64, 1024), jnp.int16),
            vmem((8, 8, 1024), F32),
            vmem((2, 8, 64, LEAD), jnp.int16),
            vmem((2, 8, 8, LEAD), F32),
            vmem((LEAD, PANEL), F32),
            vmem((8, 32, PANEL), F32),
            vmem((2, LEAD, PANEL), F32),
            vmem((PANEL, PANEL), F32),
            vmem((4, 128, 128), F32),
            vmem((PANEL, 1536), F32),
            vmem((128, 256), F32),
            dma((5,)), dma((2, 16)), dma((2,)), dma((2, 2, 3)), dma((2, 8)),
            dma((8,)), dma((8,)), dma((8,)), dma((8,)), dma((8,)), dma((8,)),
            dma((2, 8)), dma((2, 8)), dma((2, 8)), dma((2, 8)),
            dma((2, 2)), dma((2, 5)),
            dma((8,)), dma((8,)), dma((8,)), dma((8,)), dma, dma, dma((8,)), dma((8,)),
        ],
        compiler_params=pltpu.CompilerParams(
            collective_id=0, has_side_effects=True, vmem_limit_bytes=60 << 20
        ),
    )(touches, vectors, primal, dual_inverse)


def solution(mesh):
    in_specs = (
        P("cone", "con", None),
        P("cone", None, None),
        P("cone", None, None),
        P("cone", None),
    )
    out_specs = P("cone", "con")
    return jax.shard_map(shards, mesh=mesh, in_specs=in_specs, out_specs=out_specs, check_vma=False)
```

```python
import jax
import jax.numpy as jnp
from jax import lax
from jax.experimental import pallas as pl
from jax.experimental.pallas import tpu as pltpu
from jax.sharding import PartitionSpec as P

PANEL = 512
LEAD = 256
HI = lax.Precision.HIGHEST
F32 = jnp.float32
BF16 = jnp.bfloat16
MESH = pl.DeviceIdType.MESH
OFFSETS = ((0, 1), (0, 3), (1, 0), (0, 2), (1, 1), (1, 3), (1, 2), (0, 0))
PART = 128
HALF_ROWS = 2048


def tdot(a, b):
    return lax.dot_general(
        a, b, (((0,), (0,)), ((), ())), precision=HI, preferred_element_type=F32
    )


def hdot(a, b):
    return lax.dot_general(
        a, b, (((1,), (0,)), ((), ())), precision=HI, preferred_element_type=F32
    )


def micro(block, first):
    d = {}
    for j in range(8):
        column = jnp.broadcast_to(block[:, first + j : first + j + 1], (8, 128))
        for i in range(j, 8):
            d[i, j] = jnp.broadcast_to(column[i : i + 1, :], (8, 128))
    rows = [
        [jnp.broadcast_to(block[i : i + 1, h * 128 : (h + 1) * 128], (8, 128)) for h in range(2)]
        for i in range(8)
    ]
    for j in range(8):
        inverse = lax.rsqrt(d[j, j])
        low = {i: d[i, j] * inverse for i in range(j + 1, 8)}
        rows[j] = [x * inverse for x in rows[j]]
        for k in range(j + 1, 8):
            for i in range(k, 8):
                d[i, k] = d[i, k] - low[i] * low[k]
        for i in range(j + 1, 8):
            rows[i] = [x - low[i] * y for x, y in zip(rows[i], rows[j])]
    place = lax.broadcasted_iota(jnp.int32, (8, 128), 0)
    halves = []
    for h in range(2):
        upper = rows[0][h]
        for i in range(1, 8):
            upper = jnp.where(place == i, rows[i][h], upper)
        halves.append(upper)
    return jnp.concatenate(halves, axis=1)


def diagonal_factor(work):
    for p in range(16):
        upper = micro(work[8 * p : 8 * p + 8, :], 8 * p)
        work[8 * p : 8 * p + 8, :] = upper
        low = 8 * (p + 1)
        if p < 15:
            change = tdot(upper[:, :128], upper)
            work[low:, :] = work[low:, :] - change[low:, :]


def block(i):
    return pl.ds(pl.multiple_of(i * 128, 128), 128)


def factor_step(k, A, inverses, work):
    square = (128, 128)
    eye = lax.broadcasted_iota(jnp.int32, square, 0) == lax.broadcasted_iota(jnp.int32, square, 1)
    here = block(k)
    work[:, :128] = A[here, here]
    work[:, 128:] = eye.astype(F32)
    diagonal_factor(work)
    inverses[k] = work[:, 128:]
    A[here, :] = hdot(work[:, 128:], A[here, :])

    @pl.loop(k + 1, 4)
    def _(r):
        A[block(r), :] = A[block(r), :] - tdot(A[here, block(r)], A[here, :])


def substitute(A, inverses, X):
    @pl.loop(0, 4)
    def _(k):
        here = block(k)
        X[here, :] = hdot(inverses[k], X[here, :])

        @pl.loop(k + 1, 4)
        def _(r):
            X[block(r), :] = X[block(r), :] - tdot(A[here, block(r)], X[here, :])


def encode(h, chunk):
    rows, columns = h.shape
    cut = h.reshape(rows // chunk, chunk, columns)
    peak = jnp.max(jnp.abs(cut), axis=1)
    inverse = jnp.where(peak > 1e-33, 32767.0 / jnp.maximum(peak, 1e-33), 0.0)
    coded = jnp.round(cut * inverse[:, None, :]).astype(jnp.int16)
    return coded.reshape(rows, columns), peak * (1.0 / 32767.0)


def decode(coded, scale, chunk):
    rows, columns = coded.shape
    cut = coded.astype(F32).reshape(rows // chunk, chunk, columns)
    return (cut * scale[:, None, :]).reshape(rows, columns)


def kernel(
    t_ref, v_hbm, p_hbm, d_hbm, out_ref,
    rows, V, Pm, Dm, rp, rd, sendq, recvq, ssc, rsc, acc, psc, pqr, pscr,
    agq, ags, spq, sps, bpart, brecv, bfull, A, inverses, X, work,
    load_sem, g_recv, g_x, g_z, g_s, pr_send, prs_send, pr_recv, prs_recv, ag_send, ag_recv,
    bq_send, bs_send, bq_recv, bs_recv, c_recv, c_send,
    br_send, br_recv, ba_send, ba_recv, bx_send, bx_recv, ags_send, ags_recv,
):
    c = lax.axis_index("cone")
    b = lax.axis_index("con")
    z = b // 4
    xh = (b // 2) % 2
    core = b % 2
    x_peer = b + 2 - 4 * xh
    sibling = b + 1 - 2 * core
    z_peers = [lax.rem(b + 4 * k, 16) for k in (1, 2, 3)]

    leads = [
        pltpu.make_async_copy(
            v_hbm.at[0, pl.ds(PART * h, PART), :],
            rows.at[pl.ds(HALF_ROWS * h + PART * b, PART), :],
            load_sem.at[3 + h],
        )
        for h in range(2)
    ]
    loads = [
        pltpu.make_async_copy(h.at[0], m, load_sem.at[k])
        for k, (h, m) in enumerate(((p_hbm, Pm), (d_hbm, Dm), (v_hbm, V)))
    ]
    for load in leads + loads:
        load.start()

    barrier = pltpu.get_barrier_semaphore()
    for peer in [x_peer, sibling] + z_peers:
        pl.semaphore_signal(barrier, inc=1, device_id={"con": peer}, device_id_type=MESH)
    for s in range(1, 8):
        pl.semaphore_signal(
            barrier, inc=1, device_id={"cone": lax.rem(c + s, 8)}, device_id_type=MESH
        )
    pl.semaphore_wait(barrier, 12)

    def block_copy(slot, h, sem, peer):
        ref = rows.at[pl.ds(pl.multiple_of(HALF_ROWS * h + PART * slot, PART), PART), :]
        return pltpu.make_async_remote_copy(
            src_ref=ref, dst_ref=ref, send_sem=sem, recv_sem=g_recv.at[h, slot],
            device_id={"con": peer}, device_id_type=MESH,
        )

    def to_x(h):
        return block_copy(b, h, g_x.at[h], x_peer)

    def to_sibling(slot, h):
        return block_copy(slot, h, g_s.at[h, slot // 2], sibling)

    def to_z(slot, h, which):
        return [block_copy(slot, h, g_z.at[h, which, k], z_peers[k]) for k in range(3)]

    def send_on(slot, h, which):
        for copy in to_z(slot, h, which):
            copy.start()
        to_sibling(slot, h).start()

    def take_x(h):
        block_copy(x_peer, h, g_x.at[h], x_peer).wait_recv()
        send_on(x_peer, h, 1)

    def arrive(a, h):
        @pl.when(a // 2 != z)
        def _():
            slot = 2 * a + core
            block_copy(slot, h, g_x.at[h], x_peer).wait_recv()
            to_sibling(slot, h).start()

    def arrive_sibling(a, h):
        block_copy(2 * a + 1 - core, h, g_x.at[h], x_peer).wait_recv()

    own_flag = t_ref[0, b].astype(F32)

    own_chip = b // 2
    contract = (((1,), (1,)), ((), ()))

    def products(a, h, low, high):
        here = pl.ds(pl.multiple_of(HALF_ROWS * h + LEAD * a, LEAD), LEAD)

        @pl.loop(0, 4)
        def _(n):
            cs = pl.ds(pl.multiple_of(n * 256, 256), 256)
            for matrix, result in ((Pm, rp), (Dm, rd)):
                value = jnp.dot(rows[here, :], matrix[:, cs], preferred_element_type=F32)
                result[low : low + PART, cs] = value[:PART].astype(BF16)
                result[high : high + PART, cs] = value[PART:].astype(BF16)

    def grams(a, count, sink):
        first = t_ref[0, 2 * a].astype(F32) * own_flag
        second = t_ref[0, 2 * a + 1].astype(F32) * own_flag
        place = lax.broadcasted_iota(jnp.int32, (count, 256), 0)
        flags = jnp.where(place < count // 2, first, second)

        @pl.loop(0, 4)
        def _(n):
            cs = pl.ds(pl.multiple_of(n * 256, 256), 256)
            gp = lax.dot_general(rp[:count, :], V[cs, :], contract, preferred_element_type=F32)
            gd = lax.dot_general(rd[:count, :], V[cs, :], contract, preferred_element_type=F32)
            sink(cs, gp * gd * flags)

    def piece(i, size):
        return pl.ds(pl.multiple_of(i * size, size), size)

    def pivot_part():
        half = piece(core, LEAD)
        row_flag = t_ref[0, core].astype(F32)
        place = lax.broadcasted_iota(jnp.int32, (LEAD, PANEL), 1)
        flags = jnp.where(place < LEAD, t_ref[0, 0].astype(F32), t_ref[0, 1].astype(F32)) * row_flag
        lead_rows = jnp.concatenate(
            [rows[HALF_ROWS * h + PART * k : HALF_ROWS * h + PART * (k + 1), :]
             for k in range(2) for h in range(2)],
            axis=0,
        )
        gp = lax.dot_general(rp[half, :], lead_rows, contract, preferred_element_type=F32)
        gd = lax.dot_general(rd[half, :], lead_rows, contract, preferred_element_type=F32)
        bpart[...] = gp * gd * flags

    def pivot_copy(s, slot):
        peer = lax.rem(c + s, 8)
        return pltpu.make_async_remote_copy(
            src_ref=bpart.at[piece(peer, 32), :], dst_ref=brecv.at[slot],
            send_sem=br_send.at[s], recv_sem=br_recv.at[slot],
            device_id={"cone": peer}, device_id_type=MESH,
        )

    def pivot_sum_copy(s, slot):
        ref = bfull.at[core, piece(slot, 32), :]
        return pltpu.make_async_remote_copy(
            src_ref=ref, dst_ref=ref, send_sem=ba_send.at[s], recv_sem=ba_recv.at[slot],
            device_id={"cone": lax.rem(c + s, 8)}, device_id_type=MESH,
        )

    def pivot_half_copy(half):
        ref = bfull.at[half]
        return pltpu.make_async_remote_copy(
            src_ref=ref, dst_ref=ref, send_sem=bx_send, recv_sem=bx_recv,
            device_id={"con": sibling}, device_id_type=MESH,
        )

    def panel_sink(cs, h):
        X[:, cs] = h
        coded, scale = encode(h, 8)
        sendq[0, :, cs] = coded
        psc[:, cs] = scale

    def panel_copy(s, slot):
        peer = lax.rem(c + s, 8)
        return (
            pltpu.make_async_remote_copy(
                src_ref=sendq.at[0, piece(peer, 64), :], dst_ref=pqr.at[slot],
                send_sem=pr_send.at[s], recv_sem=pr_recv.at[slot],
                device_id={"cone": peer}, device_id_type=MESH,
            ),
            pltpu.make_async_remote_copy(
                src_ref=psc.at[piece(peer, 8), :], dst_ref=pscr.at[slot],
                send_sem=prs_send.at[s], recv_sem=prs_recv.at[slot],
                device_id={"cone": peer}, device_id_type=MESH,
            ),
        )

    def sum_copy(s, slot):
        peer = lax.rem(c + s, 8)
        return (
            pltpu.make_async_remote_copy(
                src_ref=agq.at[slot], dst_ref=agq.at[slot],
                send_sem=ag_send.at[s], recv_sem=ag_recv.at[slot],
                device_id={"cone": peer}, device_id_type=MESH,
            ),
            pltpu.make_async_remote_copy(
                src_ref=ags.at[slot], dst_ref=ags.at[slot],
                send_sem=ags_send.at[s], recv_sem=ags_recv.at[slot],
                device_id={"cone": peer}, device_id_type=MESH,
            ),
        )

    def bulk_copy(a, slot, h, part=None):
        here = piece(h, LEAD) if part is None else piece(2 * h + part, PART)
        scales = piece(h, 8)
        return (
            pltpu.make_async_remote_copy(
                src_ref=sendq.at[a, here, :], dst_ref=recvq.at[slot, here, :],
                send_sem=bq_send.at[h, a], recv_sem=bq_recv.at[h, slot],
                device_id={"cone": a}, device_id_type=MESH,
            ),
            pltpu.make_async_remote_copy(
                src_ref=ssc.at[a, scales, :], dst_ref=rsc.at[slot, scales, :],
                send_sem=bs_send.at[h, a], recv_sem=bs_recv.at[h, slot],
                device_id={"cone": a}, device_id_type=MESH,
            ),
        )

    def compute(a, h):
        here = piece(h, LEAD)

        def sink(cs, value):
            @pl.when(a == c)
            def _():
                acc[here, cs] = value

            @pl.when(a != c)
            def _():
                coded, scale = encode(value, 32)
                sendq[a, here, cs] = coded
                ssc[a, piece(h, 8), cs] = scale

        arrive_sibling(a, h)
        products(a, h, 0, PART)
        grams(a, LEAD, sink)

    def target(t):
        dx = dy = 0
        for k, (x, y) in enumerate(OFFSETS):
            dx = jnp.where(t == k + 1, x, dx)
            dy = jnp.where(t == k + 1, y, dy)
        return lax.rem(c // 4 + dx, 2) * 4 + lax.rem(lax.rem(c, 4) + dy, 4)

    def issue(low, high, h):
        for part in range(2):
            for t in range(low, high):
                a = target(t)

                @pl.when(a != 0)
                def _():
                    coded, scale = bulk_copy(a, c, h, part)
                    if part == 0:
                        scale.start()
                    coded.start()

    def bulk(low, high, h):
        @pl.loop(low, high)
        def _(t):
            a = target(t)

            @pl.when(a != 0)
            def _():
                compute(a, h)

            if h == 1:
                @pl.when(t == 3)
                def _():
                    issue(1, 4, h)

            if h == 1:
                @pl.when(t == 7)
                def _():
                    issue(4, 8, h)

    def arrive_all(h):
        @pl.loop(1, 8)
        def _(a):
            arrive(a, h)

    def accumulate(h):
        @pl.loop(1, 8)
        def _(s):
            source = lax.rem(c + s, 8)
            for copy in bulk_copy(source, source, h):
                copy.wait_recv()
            for r in range(2):
                part = piece(2 * h + r, PART)
                scales = rsc[source, piece(h, 8), :]
                acc[part, :] = acc[part, :] + decode(
                    recvq[source, part, :], scales[4 * r : 4 * r + 4], 32
                )

    def spread_copy(slot, place, peer):
        return [
            pltpu.make_async_remote_copy(
                src_ref=ref.at[slot], dst_ref=ref.at[slot],
                send_sem=c_send.at[kind, place], recv_sem=c_recv.at[kind, slot],
                device_id={"con": peer}, device_id_type=MESH,
            )
            for kind, ref in enumerate((spq, sps))
        ]

    at_home_z = z == c // 2
    at_home_x = xh == lax.rem(c, 2)

    def spread_take(slot):
        for copy in spread_copy(slot, 0, sibling):
            copy.wait_recv()

    def spread_send(place, peer, sent=False):
        for copy in spread_copy(core, place, peer):
            if sent:
                copy.wait_send()
            else:
                copy.start()

    def spread_on():
        for k in range(3):
            spread_send(2 + k, z_peers[k])
        spread_send(0, sibling)

    def spread_start():
        @pl.when(at_home_z & at_home_x)
        def _():
            spq[core] = agq[:, :, :LEAD]
            sps[core] = ags[:, :, :LEAD]
            spread_send(1, x_peer)
            spread_on()

    def spread_relay():
        @pl.when(at_home_z & (xh != lax.rem(c, 2)))
        def _():
            spread_take(core)
            spread_on()

    def spread_relay_far():
        @pl.when(z != c // 2)
        def _():
            spread_take(core)
            spread_send(0, sibling)

    def spread_end():
        spread_send(0, sibling, sent=True)

        @pl.when(at_home_z)
        def _():
            for k in range(3):
                spread_send(2 + k, z_peers[k], sent=True)

        @pl.when(at_home_z & at_home_x)
        def _():
            spread_send(1, x_peer, sent=True)

    for lead in leads:
        lead.wait()
    for h in range(2):
        to_x(h).start()
    send_on(b, 0, 0)

    @pl.when(own_chip == 0)
    def _():
        send_on(b, 1, 0)

    for load in loads:
        load.wait()
    take_x(0)

    @pl.when(x_peer // 2 == 0)
    def _():
        take_x(1)

    for h in range(2):
        arrive(0, h)
    for h in range(2):
        arrive_sibling(0, h)
        products(0, h, PART * h, LEAD + PART * h)
    pivot_part()
    for s in range(1, 8):
        pivot_copy(s, c).start()

    grams(0, PANEL, panel_sink)
    for s in range(1, 8):
        for copy in panel_copy(s, c):
            copy.start()
    arrive_all(0)

    @pl.when(own_chip != 0)
    def _():
        send_on(b, 1, 0)

    @pl.when(x_peer // 2 != 0)
    def _():
        take_x(1)

    half_piece = piece(c, 32)
    bfull[core, half_piece, :] = bpart[half_piece, :]

    @pl.loop(1, 8)
    def _(s):
        source = lax.rem(c + s, 8)
        pivot_copy(s, source).wait_recv()
        bfull[core, half_piece, :] = bfull[core, half_piece, :] + brecv[source]

    for s in range(1, 8):
        pivot_sum_copy(s, c).start()

    bulk(1, 4, 0)

    for s in range(1, 8):
        pivot_sum_copy(s, lax.rem(c + s, 8)).wait_recv()
    pivot_half_copy(core).start()

    mine = piece(c, 64)

    @pl.loop(1, 8)
    def _(s):
        source = lax.rem(c + s, 8)
        for copy in panel_copy(s, source):
            copy.wait_recv()
        X[mine, :1024] = X[mine, :1024] + decode(pqr[source], pscr[source], 8)

    agq[c], ags[c] = encode(X[mine, :1024], 8)
    for s in range(1, 8):
        for copy in sum_copy(s, c):
            copy.start()

    issue(1, 4, 0)
    bulk(4, 9, 0)
    arrive_all(1)

    for s in range(1, 8):
        for copy in sum_copy(s, lax.rem(c + s, 8)):
            copy.wait_recv()
    spread_start()
    issue(4, 8, 0)

    @pl.loop(0, 8)
    def _(s):
        X[piece(s, 64), :1024] = decode(agq[s], ags[s], 8)

    pivot_half_copy(1 - core).wait_recv()
    A[:LEAD, :] = bfull[0]
    A[LEAD:, :] = bfull[1]
    A[...] = (A[...] + A[...].T) * 0.5

    @pl.loop(0, 4)
    def _(k):
        low = jnp.where(k == 0, 1, jnp.where(k == 1, 4, 9))
        high = jnp.where(k == 0, 4, 9)
        bulk(low, high, 1)
        factor_step(k, A, inverses, work)

        @pl.when(k == 0)
        def _():
            spread_relay()

        @pl.when(k == 1)
        def _():
            spread_relay_far()

    @pl.when(c != 0)
    def _():
        accumulate(0)

    spread_take(1 - core)

    @pl.loop(0, 8)
    def _(s):
        for slot in range(2):
            low = 1024 + slot * LEAD
            X[piece(s, 64), low : low + LEAD] = decode(spq[slot, s], sps[slot, s], 8)

    substitute(A, inverses, X)

    @pl.when(c != 0)
    def _():
        accumulate(1)

        @pl.loop(0, 4)
        def _(q):
            r = 2 * (q % 2) + q // 2
            change = tdot(X[:, block(8 + r)], X[:, :1024])
            place = lax.broadcasted_iota(jnp.int32, (128, 1024), 1)
            gone = (place < LEAD) & (b < 2)
            out_ref[block(r), :] = jnp.where(gone, 0.0, acc[block(q), :] - change)

    @pl.when(c == 0)
    def _():
        out_ref[...] = X[:, :1024]

    for h in range(2):
        to_x(h).wait_send()
        for copy in to_z(b, h, 0) + to_z(x_peer, h, 1):
            copy.wait_send()

        @pl.loop(0, 8)
        def _(a):
            to_sibling(2 * a + core, h).wait_send()

    for s in range(1, 8):
        for copy in panel_copy(s, c) + sum_copy(s, c):
            copy.wait_send()

        a = lax.rem(c + s, 8)

        @pl.when(a != 0)
        def _():
            for h in range(2):
                for copy in bulk_copy(a, c, h):
                    copy.wait_send()

        pivot_copy(s, c).wait_send()
        pivot_sum_copy(s, c).wait_send()

    pivot_half_copy(core).wait_send()
    spread_end()


def shards(vectors, primal, dual_inverse, touches):
    dma = pltpu.SemaphoreType.DMA
    vmem = pltpu.VMEM
    anywhere = pl.BlockSpec(memory_space=pl.ANY)
    return pl.pallas_call(
        kernel,
        out_shape=jax.ShapeDtypeStruct((PANEL, 1024), F32),
        in_specs=[pl.BlockSpec(memory_space=pltpu.SMEM), anywhere, anywhere, anywhere],
        out_specs=pl.BlockSpec(memory_space=pltpu.VMEM),
        scratch_shapes=[
            vmem((4096, 1024), BF16),
            vmem((1024, 1024), BF16),
            vmem((1024, 1024), BF16),
            vmem((1024, 1024), BF16),
            vmem((PANEL, 1024), BF16),
            vmem((PANEL, 1024), BF16),
            vmem((8, PANEL, 1024), jnp.int16),
            vmem((8, PANEL, 1024), jnp.int16),
            vmem((8, 16, 1024), F32),
            vmem((8, 16, 1024), F32),
            vmem((PANEL, 1024), F32),
            vmem((64, 1024), F32),
            vmem((8, 64, 1024), jnp.int16),
            vmem((8, 8, 1024), F32),
            vmem((8, 64, 1024), jnp.int16),
            vmem((8, 8, 1024), F32),
            vmem((2, 8, 64, LEAD), jnp.int16),
            vmem((2, 8, 8, LEAD), F32),
            vmem((LEAD, PANEL), F32),
            vmem((8, 32, PANEL), F32),
            vmem((2, LEAD, PANEL), F32),
            vmem((PANEL, PANEL), F32),
            vmem((4, 128, 128), F32),
            vmem((PANEL, 1536), F32),
            vmem((128, 256), F32),
            dma((5,)), dma((2, 16)), dma((2,)), dma((2, 2, 3)), dma((2, 8)),
            dma((8,)), dma((8,)), dma((8,)), dma((8,)), dma((8,)), dma((8,)),
            dma((2, 8)), dma((2, 8)), dma((2, 8)), dma((2, 8)),
            dma((2, 2)), dma((2, 5)),
            dma((8,)), dma((8,)), dma((8,)), dma((8,)), dma, dma, dma((8,)), dma((8,)),
        ],
        compiler_params=pltpu.CompilerParams(
            collective_id=0, has_side_effects=True, vmem_limit_bytes=60 << 20
        ),
    )(touches, vectors, primal, dual_inverse)


def solution(mesh):
    in_specs = (
        P("cone", "con", None),
        P("cone", None, None),
        P("cone", None, None),
        P("cone", None),
    )
    out_specs = P("cone", "con")
    return jax.shard_map(shards, mesh=mesh, in_specs=in_specs, out_specs=out_specs, check_vma=False)
```
